512 devices in a mesh: seq: 128 (over z_lo, y, x), ch: 4 (over z_hi, core).
Axes of the slice: x: 4, y: 8, z: 8 (z_hi: 2, z_lo: 4; z = z_hi * 4 + z_lo), core: 2. Of those that a mesh axis runs over, the one named last changes fastest.
Arguments:
- tokens: bfloat16 [16384, 512], P('seq', 'ch'), may hold values from -36 to 36
- gain_mix: float32 [512], replicated, may hold values from 0.1 to 1.9
- w_in: bfloat16 [3, 512, 512], P(None, None, 'ch'), may hold values from -0.25 to 0.25
- short_w: float32 [3, 3, 512], P(None, None, 'ch'), may hold values from -3.5 to 3.5
- filters: bfloat16 [2, 512, 16384], P(None, 'ch', 'seq'), may hold values from -0.046875 to 0.046875
- conv_bias: float32 [2, 512], P(None, 'ch'), may hold values from 0.5 to 1.5
- w_out: bfloat16 [512, 512], P('ch'), may hold values from -0.25 to 0.25
- gain_mlp: float32 [512], replicated, may hold values from 0.1 to 1.9
- w_up: bfloat16 [512, 2048], P(None, 'ch'), may hold values from -0.25 to 0.25
- w_down: bfloat16 [2048, 512], P('ch'), may hold values from -0.125 to 0.125
Outputs:
- result: bfloat16 [16384, 512], P('seq', 'ch')
The draws below stay inside these ranges and needn't reach their ends.
All inputs are finite; a program needn't handle non-finite values.
Results may differ from the reference program's by a relative error of at most 0.018.
Values may be sent and summed in bfloat16 or wider, within the bound.
No kernel may reach another device: no remote copies, remote signals or barrier semaphores. Data moves between devices by JAX's collectives and lax.ppermute only.
A program may use at most 64 MiB of HBM per device.

```python
import math
import jax
import jax.numpy as jnp
from jax import lax

D = 512
FF = 2048
ORDER = 2
SHORT = 3
L = 16384


def draw_tokens(key, part):
    key = jax.random.fold_in(key, 11)
    key_rows, key_cols, key_base = jax.random.split(key, 3)
    rows = jnp.exp(jax.random.uniform(key_rows, (L, 1), jnp.float32, math.log(0.3), math.log(3.0)))
    cols = jnp.exp(jax.random.uniform(key_cols, (1, D), jnp.float32, math.log(0.3), math.log(3.0)))
    base = jnp.clip(jax.random.normal(key_base, (L, D), jnp.float32), -4.0, 4.0)
    return (base * rows * cols).astype(jnp.bfloat16)


def block_levels(rng, extent, cuts, smallest, largest):
    level = 1.0
    for axis_at, parts in cuts:
        steps = jax.random.uniform(jax.random.fold_in(jax.random.fold_in(rng, 6), axis_at), (parts,), jnp.float32, smallest / len(cuts), largest / len(cuts))
        level = level * jnp.repeat(jnp.exp(steps), extent[axis_at] // parts).reshape((-1,) + (1,) * (len(extent) - 1 - axis_at))
    return level


def scatter_about(key, dims, spread, limit, pieces=(), dtype=jnp.bfloat16):
    level = block_levels(key, dims, pieces, -0.22, 0.18) if pieces else 1.0
    array = jax.random.normal(key, dims, jnp.float32) * spread * level
    return jnp.minimum(jnp.maximum(array, -limit), limit).astype(dtype)


def setup_inputs(seed: int = 0) -> dict:
    streams_of = jax.random.split(jax.random.key(seed), 11)
    tokens = draw_tokens(jax.random.fold_in(streams_of[10], 71), 0)
    gain_mix = jnp.clip(1.0 + 0.18 * jax.random.normal(streams_of[1], (D,), jnp.float32), 0.1, 1.9)
    w_in = scatter_about(streams_of[2], (ORDER + 1, D, D), D ** -0.5, 0.25, ((2, 4),))
    short_w = scatter_about(streams_of[3], (ORDER + 1, SHORT, D), SHORT ** -0.5, 3.5, ((2, 4),), jnp.float32)
    filters = scatter_about(streams_of[4], (ORDER, D, L), L ** -0.5, 0.046875, ((1, 4), (2, 128)))
    conv_bias = jnp.clip(0.5 + 1.0 * jax.random.uniform(streams_of[5], (ORDER, D), jnp.float32) ** block_levels(streams_of[5], (ORDER, D), ((1, 4),), -0.2, 0.2), 0.5, 1.5)
    w_out = scatter_about(streams_of[6], (D, D), D ** -0.5, 0.25, ((0, 4),))
    gain_mlp = jnp.clip(1.0 + 0.18 * jax.random.normal(streams_of[7], (D,), jnp.float32), 0.1, 1.9)
    w_up = scatter_about(streams_of[8], (D, FF), D ** -0.5, 0.25, ((1, 4),))
    w_down = scatter_about(streams_of[9], (FF, D), FF ** -0.5, 0.125, ((0, 4),))
    return {"tokens": tokens, "gain_mix": gain_mix, "w_in": w_in, "short_w": short_w, "filters": filters, "conv_bias": conv_bias, "w_out": w_out, "gain_mlp": gain_mlp, "w_up": w_up, "w_down": w_down}


epsilon = 1e-06

def rms_norm(values, gain):
    wide = values.astype(jnp.float32)
    scale = lax.rsqrt(lax.optimization_barrier(jnp.mean(wide * wide, axis=-1, keepdims=True)) + epsilon)
    return (wide * scale * gain).astype(jnp.bfloat16)

def long_conv(signal, response, bias):
    length = signal.shape[0]
    size = 2 * length
    spectrum = jnp.fft.rfft(signal, n=size, axis=0) * jnp.fft.rfft(response, n=size, axis=0)
    return jnp.fft.irfft(spectrum, n=size, axis=0)[:length] + bias[None, :] * signal

def reference(tokens, gain_mix, w_in, short_w, filters, conv_bias, w_out, gain_mlp, w_up, w_down):
    length = tokens.shape[0]
    normed = rms_norm(tokens, gain_mix)
    projected = jnp.stack([jnp.dot(normed, w_in[k], preferred_element_type=jnp.float32) for k in range(w_in.shape[0])]).astype(jnp.bfloat16)
    padded = jnp.pad(projected.astype(jnp.float32), ((0, 0), (SHORT - 1, 0), (0, 0)))
    smoothed = jnp.zeros(projected.shape, jnp.float32)
    for shift in range(SHORT):
        start = SHORT - 1 - shift
        smoothed = smoothed + short_w[:, shift, None, :] * padded[:, start:start + length, :]
    smoothed = smoothed.astype(jnp.bfloat16)
    first = long_conv(smoothed[0].astype(jnp.float32), filters[0].T.astype(jnp.float32), conv_bias[0]).astype(jnp.bfloat16)
    first = lax.optimization_barrier(first)
    gated = (smoothed[1].astype(jnp.float32) * first.astype(jnp.float32)).astype(jnp.bfloat16)
    second = long_conv(gated.astype(jnp.float32), filters[1].T.astype(jnp.float32), conv_bias[1]).astype(jnp.bfloat16)
    second = lax.optimization_barrier(second)
    mixed = (smoothed[2].astype(jnp.float32) * second.astype(jnp.float32)).astype(jnp.bfloat16)
    middle = (tokens.astype(jnp.float32) + jnp.dot(mixed, w_out, preferred_element_type=jnp.float32)).astype(jnp.bfloat16)
    normed_mlp = rms_norm(middle, gain_mlp)
    hidden = jax.nn.gelu(jnp.dot(normed_mlp, w_up, preferred_element_type=jnp.float32)).astype(jnp.bfloat16)
    return (middle.astype(jnp.float32) + jnp.dot(hidden, w_down, preferred_element_type=jnp.float32)).astype(jnp.bfloat16)
```

```python
import math

import jax
import jax.numpy as jnp
from jax import lax
from jax.sharding import Mesh, PartitionSpec as P

epsilon = 1e-06

SEQ = ("z", "y", "x")
CH = ("h", "c")


def rms_norm(values, gain):
    wide = values.astype(jnp.float32)
    scale = lax.rsqrt(jnp.mean(wide * wide, axis=-1, keepdims=True) + epsilon)
    return (wide * scale * gain).astype(jnp.bfloat16)


def transform_tables(rows, cols):
    size = rows * cols
    row_index = jnp.arange(rows, dtype=jnp.int32)
    col_index = jnp.arange(cols, dtype=jnp.int32)
    row_angle = (row_index[:, None] * row_index[None, :] % rows).astype(jnp.float32) * (
        2.0 * math.pi / rows
    )
    col_angle = (col_index[:, None] * col_index[None, :] % cols).astype(jnp.float32) * (
        2.0 * math.pi / cols
    )
    twist_angle = (row_index[:, None] * col_index[None, :] % size).astype(jnp.float32) * (
        2.0 * math.pi / size
    )
    return (
        jnp.cos(row_angle),
        jnp.sin(row_angle),
        jnp.cos(col_angle),
        jnp.sin(col_angle),
        jnp.cos(twist_angle),
        jnp.sin(twist_angle),
    )


def product(form, left, right):
    return jnp.einsum(form, left, right, precision=lax.Precision.HIGHEST)


def forward_grid(grid, tables):
    row_cos, row_sin, col_cos, col_sin, twist_cos, twist_sin = tables
    half = grid.shape[1]
    first_real = product("ka,cab->ckb", row_cos[:, :half], grid)
    first_imag = -product("ka,cab->ckb", row_sin[:, :half], grid)
    turned_real = first_real * twist_cos + first_imag * twist_sin
    turned_imag = first_imag * twist_cos - first_real * twist_sin
    out_real = product("ckb,bm->ckm", turned_real, col_cos) + product(
        "ckb,bm->ckm", turned_imag, col_sin
    )
    out_imag = product("ckb,bm->ckm", turned_imag, col_cos) - product(
        "ckb,bm->ckm", turned_real, col_sin
    )
    return (out_real, out_imag)


def inverse_grid(spec_real, spec_imag, tables):
    row_cos, row_sin, col_cos, col_sin, twist_cos, twist_sin = tables
    rows = row_cos.shape[0]
    half = rows // 2
    size = rows * col_cos.shape[0]
    inner_real = product("ckm,mb->ckb", spec_real, col_cos) - product(
        "ckm,mb->ckb", spec_imag, col_sin
    )
    inner_imag = product("ckm,mb->ckb", spec_real, col_sin) + product(
        "ckm,mb->ckb", spec_imag, col_cos
    )
    turned_real = inner_real * twist_cos - inner_imag * twist_sin
    turned_imag = inner_real * twist_sin + inner_imag * twist_cos
    outer = product("dk,ckb->cdb", row_cos[:half], turned_real) - product(
        "dk,ckb->cdb", row_sin[:half], turned_imag
    )
    return outer / size


def long_conv(signal, response, bias, tables):
    channels, length = signal.shape
    rows = tables[0].shape[0]
    cols = tables[2].shape[0]
    signal_wide = signal.astype(jnp.float32)
    sig_real, sig_imag = forward_grid(signal_wide.reshape(channels, rows // 2, cols), tables)
    res_real, res_imag = forward_grid(
        response.astype(jnp.float32).reshape(channels, rows // 2, cols), tables
    )
    prod_real = sig_real * res_real - sig_imag * res_imag
    prod_imag = sig_real * res_imag + sig_imag * res_real
    filtered = inverse_grid(prod_real, prod_imag, tables).reshape(channels, length)
    return (filtered + bias[:, None] * signal_wide).astype(jnp.bfloat16)


def apply_gate(gate, signal):
    signal = lax.optimization_barrier(signal)
    return (gate.astype(jnp.float32) * signal.astype(jnp.float32)).astype(jnp.bfloat16)


def other_half_pairs():
    pairs = []
    for z in range(8):
        there = (z + 2) % 8
        if there // 4 == z // 4:
            there = (z - 2) % 8
        pairs.append((z % 4 * 2 + z // 4, there % 4 * 2 + there // 4))
    return pairs


def whole_w_out(w_out):
    other = lax.ppermute(w_out, ("z", "h"), other_half_pairs())
    low = lax.axis_index("h") == 0
    halves = jnp.stack([jnp.where(low, w_out, other), jnp.where(low, other, w_out)], axis=1)
    return lax.all_gather(halves, "c", axis=0).reshape(-1, w_out.shape[1])


def channel_work(u, taps, bias, samples):
    length = u.shape[1]
    signals = u[:3].astype(jnp.float32)
    order = taps.shape[1]
    padded = jnp.pad(signals, ((0, 0), (order - 1, 0)))
    smoothed = jnp.zeros(signals.shape, jnp.float32)
    for shift in range(order):
        start = order - 1 - shift
        smoothed = smoothed + taps[:, shift, None] * padded[:, start : start + length]
    smoothed = smoothed.astype(jnp.bfloat16)
    tables = transform_tables(2 * samples, length // samples)
    first = long_conv(smoothed[0:1], u[3:4], bias[0:1], tables)
    gated = apply_gate(smoothed[1:2], first)
    second = long_conv(gated, u[4:5], bias[1:2], tables)
    return apply_gate(smoothed[2:3], second)[0]


def local(tokens, gain_mix, w_in, short_w, filters, conv_bias, w_out, gain_mlp, w_up, w_down):
    samples, width = tokens.shape
    shards = lax.axis_size(SEQ)
    whole = lax.all_gather(tokens, CH, axis=1, tiled=True)
    normed = rms_norm(whole, gain_mix)
    projected = jnp.einsum("td,kde->ekt", normed, w_in, preferred_element_type=jnp.float32).astype(
        jnp.bfloat16
    )
    outgoing = jnp.concatenate([projected, filters.transpose(1, 0, 2)], axis=1)
    arrived = lax.all_to_all(outgoing, SEQ, split_axis=0, concat_axis=0, tiled=True)
    w_out_whole = whole_w_out(w_out)
    mine = lax.axis_index(SEQ)
    taps = lax.dynamic_index_in_dim(short_w, mine, 2, keepdims=False)
    bias = lax.dynamic_index_in_dim(conv_bias, mine, 1, keepdims=False)
    mixed = channel_work(arrived.transpose(1, 0, 2).reshape(5, -1), taps, bias, samples)
    doubled = jnp.repeat(mixed.reshape(shards, samples), 2, axis=0)
    returned = lax.all_to_all(doubled, SEQ + ("h",), split_axis=0, concat_axis=0, tiled=True)
    both = lax.all_gather(returned, "c", axis=0, tiled=True)
    share = lax.dot_general(
        both, w_out_whole, (((0,), (0,)), ((), ())), preferred_element_type=jnp.float32
    )
    middle = (whole.astype(jnp.float32) + share).astype(jnp.bfloat16)
    normed_mlp = rms_norm(middle, gain_mlp)
    hidden = jax.nn.gelu(jnp.dot(normed_mlp, w_up, preferred_element_type=jnp.float32)).astype(
        jnp.bfloat16
    )
    partial = jnp.dot(hidden, w_down, preferred_element_type=jnp.float32).astype(jnp.bfloat16)
    pieces = partial.reshape(samples, -1, width).transpose(1, 0, 2)
    pieces = lax.all_to_all(pieces, CH, split_axis=0, concat_axis=0, tiled=True)
    total = jnp.sum(pieces.astype(jnp.float32), axis=0)
    own = lax.dynamic_slice_in_dim(middle, lax.axis_index(CH) * width, width, 1)
    return (own.astype(jnp.float32) + total).astype(jnp.bfloat16)


def solution(mesh):
    fine = Mesh(mesh.devices.reshape(4, 8, 4, 2, 2), SEQ + CH)
    return jax.shard_map(
        local,
        mesh=fine,
        in_specs=(
            P(SEQ, CH),
            P(),
            P(None, None, CH),
            P(None, None, CH),
            P(None, CH, SEQ),
            P(None, CH),
            P(CH, None),
            P(),
            P(None, CH),
            P(CH, None),
        ),
        out_specs=P(SEQ, CH),
        check_vma=False,
    )
```

```python
import jax
import jax.numpy as jnp
import ml_dtypes
import numpy as np
from jax import lax
from jax.experimental import pallas as pl
from jax.experimental.pallas import tpu as pltpu
from jax.sharding import Mesh, PartitionSpec as P

epsilon = 1e-06

SEQ = ("z", "y", "x")
CH = ("h", "c")


def rms_norm(values, gain):
    wide = values.astype(jnp.float32)
    scale = lax.rsqrt(jnp.mean(wide * wide, axis=-1, keepdims=True) + epsilon)
    return (wide * scale * gain).astype(jnp.bfloat16)


def halves_of(table):
    high = table.astype(ml_dtypes.bfloat16)
    low = (table - high.astype(np.float64)).astype(ml_dtypes.bfloat16)
    return high, low


def transform_tables(rows, cols):
    size = rows * cols
    row = np.arange(rows, dtype=np.float64)
    col = np.arange(cols, dtype=np.float64)
    outer_angle = 2.0 * np.pi * (((row[:, None] + 0.25) * row[None, :]) % rows) / rows
    inner_angle = 2.0 * np.pi * ((col[:, None] * col[None, :]) % cols) / cols
    turn_angle = 2.0 * np.pi * (row[:, None] + 0.25) * col[None, :] / size
    outer = np.concatenate([np.cos(outer_angle), -np.sin(outer_angle)], axis=0)
    cos, sin = np.cos(inner_angle), np.sin(inner_angle)
    inner = np.block([[cos, -sin], [sin, cos]])
    outer_high, outer_low = halves_of(outer)
    inner_high, inner_low = halves_of(inner)
    back_high, back_low = halves_of(outer.T / size)
    return (
        np.concatenate([outer_high, outer_low], axis=1),
        inner_high,
        inner_low,
        back_high,
        back_low,
        np.cos(turn_angle).astype(np.float32),
        -np.sin(turn_angle).astype(np.float32),
    )


def dot(left, right):
    return jnp.dot(left, right, preferred_element_type=jnp.float32)


def split(values):
    high = values.astype(jnp.bfloat16)
    return high, (values - high.astype(jnp.float32)).astype(jnp.bfloat16)


def dot_split(values, high_table, low_table):
    high, low = split(values)
    rows = values.shape[0]
    both = dot(jnp.concatenate([high, low], axis=0), high_table)
    return both[:rows] + both[rows:] + dot(high, low_table)


def delayed(values, by):
    rows, cols = values.shape
    turned = pltpu.roll(values, by, 1)
    above = pltpu.roll(turned, 1, 0)
    row = lax.broadcasted_iota(jnp.int32, (rows, cols), 0)
    col = lax.broadcasted_iota(jnp.int32, (rows, cols), 1)
    return jnp.where(col >= by, turned, jnp.where(row >= 1, above, 0.0))


def round_bf16(values):
    return values.astype(jnp.bfloat16).astype(jnp.float32)


def channel_kernel(
    scalars, u, outer, inner_high, inner_low, back_high, back_low, turn_real, turn_imag, mixed
):
    rows, cols = u.shape[1], u.shape[2]

    def short(k):
        values = u[k].astype(jnp.float32)
        total = scalars[3 * k] * values
        total = total + scalars[3 * k + 1] * delayed(values, 1)
        total = total + scalars[3 * k + 2] * delayed(values, 2)
        return total.astype(jnp.bfloat16)

    def forward(signals):
        count = len(signals)
        side = jnp.concatenate(signals, axis=1) if count > 1 else signals[0]
        first = dot(outer[...], jnp.concatenate([side, side], axis=0))
        turned = []
        for k in range(count):
            real = first[:rows, k * cols : (k + 1) * cols]
            imag = first[rows:, k * cols : (k + 1) * cols]
            turned.append(
                jnp.concatenate(
                    [
                        real * turn_real[...] - imag * turn_imag[...],
                        real * turn_imag[...] + imag * turn_real[...],
                    ],
                    axis=1,
                )
            )
        stacked = jnp.concatenate(turned, axis=0) if count > 1 else turned[0]
        spectra = dot_split(stacked, inner_high[...], inner_low[...])
        return [
            (spectra[k * rows : (k + 1) * rows, :cols], spectra[k * rows : (k + 1) * rows, cols:])
            for k in range(count)
        ]

    def inverse(one, two):
        real = one[0] * two[0] - one[1] * two[1]
        negated = -one[0] * two[1] - one[1] * two[0]
        inner = dot_split(
            jnp.concatenate([real, negated], axis=1), inner_high[...], inner_low[...]
        )
        real, negated = inner[:, :cols], inner[:, cols:]
        turned = jnp.concatenate(
            [
                real * turn_real[...] - negated * turn_imag[...],
                -negated * turn_real[...] - real * turn_imag[...],
            ],
            axis=0,
        )
        high, low = split(turned)
        side = dot(back_high[...], jnp.concatenate([high, low], axis=1))
        return side[:, :cols] + side[:, cols:] + dot(back_low[...], high)

    v = short(0)
    signal, response_one, response_two = forward([v, u[3], u[4]])
    first = inverse(signal, response_one) + scalars[9] * v.astype(jnp.float32)
    gated = (short(1).astype(jnp.float32) * round_bf16(first)).astype(jnp.bfloat16)
    (signal,) = forward([gated])
    second = inverse(signal, response_two) + scalars[10] * gated.astype(jnp.float32)
    mixed[...] = (short(2).astype(jnp.float32) * round_bf16(second)).astype(jnp.bfloat16)


def channel_work(u, scalars):
    _, rows, cols = u.shape
    tables = [jnp.asarray(table) for table in transform_tables(rows, cols)]
    vmem = pl.BlockSpec(memory_space=pltpu.VMEM)
    return pl.pallas_call(
        channel_kernel,
        out_shape=jax.ShapeDtypeStruct((rows, cols), jnp.bfloat16),
        in_specs=[pl.BlockSpec(memory_space=pltpu.SMEM)] + [vmem] * (1 + len(tables)),
        out_specs=vmem,
        compiler_params=pltpu.CompilerParams(vmem_limit_bytes=16 * 2**20),
        cost_estimate=pl.CostEstimate(flops=2**29, bytes_accessed=2**20, transcendentals=0),
    )(scalars, u, *tables)


def other_half_pairs():
    pairs = []
    for z in range(8):
        there = (z + 2) % 8
        if there // 4 == z // 4:
            there = (z - 2) % 8
        pairs.append((z % 4 * 2 + z // 4, there % 4 * 2 + there // 4))
    return pairs


def whole_w_out(w_out):
    other = lax.ppermute(w_out, ("z", "h"), other_half_pairs())
    low = lax.axis_index("h") == 0
    halves = jnp.stack([jnp.where(low, w_out, other), jnp.where(low, other, w_out)], axis=1)
    return lax.all_gather(halves, "c", axis=0).reshape(-1, w_out.shape[1])


def local(tokens, gain_mix, w_in, short_w, filters, conv_bias, w_out, gain_mlp, w_up, w_down):
    samples, width = tokens.shape
    shards = lax.axis_size(SEQ)
    whole = lax.all_gather(tokens, CH, axis=1, tiled=True)
    normed = rms_norm(whole, gain_mix)
    projected = jnp.einsum("td,kde->ekt", normed, w_in, preferred_element_type=jnp.float32).astype(
        jnp.bfloat16
    )
    outgoing = jnp.concatenate([projected, filters.transpose(1, 0, 2)], axis=1)
    arrived = lax.all_to_all(outgoing, SEQ, split_axis=0, concat_axis=0, tiled=True)
    w_out_whole = whole_w_out(w_out)
    mine = lax.axis_index(SEQ)
    scalars = lax.dynamic_index_in_dim(
        jnp.concatenate([short_w.reshape(-1, width), conv_bias], axis=0), mine, 1, keepdims=False
    )
    mixed = channel_work(arrived.transpose(1, 0, 2), scalars)
    doubled = jnp.repeat(mixed.reshape(shards, samples), 2, axis=0)
    returned = lax.all_to_all(doubled, SEQ + ("h",), split_axis=0, concat_axis=0, tiled=True)
    both = lax.all_gather(returned, "c", axis=0, tiled=True)
    share = lax.dot_general(
        both, w_out_whole, (((0,), (0,)), ((), ())), preferred_element_type=jnp.float32
    )
    middle = (whole.astype(jnp.float32) + share).astype(jnp.bfloat16)
    normed_mlp = rms_norm(middle, gain_mlp)
    hidden = jax.nn.gelu(jnp.dot(normed_mlp, w_up, preferred_element_type=jnp.float32)).astype(
        jnp.bfloat16
    )
    partial = jnp.dot(hidden, w_down, preferred_element_type=jnp.float32).astype(jnp.bfloat16)
    pieces = partial.reshape(samples, -1, width).transpose(1, 0, 2)
    pieces = lax.all_to_all(pieces, CH, split_axis=0, concat_axis=0, tiled=True)
    total = jnp.sum(pieces.astype(jnp.float32), axis=0)
    own = lax.dynamic_slice_in_dim(middle, lax.axis_index(CH) * width, width, 1)
    return (own.astype(jnp.float32) + total).astype(jnp.bfloat16)


def solution(mesh):
    fine = Mesh(mesh.devices.reshape(4, 8, 4, 2, 2), SEQ + CH)
    return jax.shard_map(
        local,
        mesh=fine,
        in_specs=(
            P(SEQ, CH),
            P(),
            P(None, None, CH),
            P(None, None, CH),
            P(None, CH, SEQ),
            P(None, CH),
            P(CH, None),
            P(),
            P(None, CH),
            P(CH, None),
        ),
        out_specs=P(SEQ, CH),
        check_vma=False,
    )
```

```python
import jax
import jax.numpy as jnp
import ml_dtypes
import numpy as np
from jax import lax
from jax.experimental import pallas as pl
from jax.experimental.pallas import tpu as pltpu
from jax.sharding import Mesh, PartitionSpec as P

epsilon = 1e-06

SEQ = ("z", "y", "x")
CH = ("h", "c")


def rms_norm(values, gain):
    wide = values.astype(jnp.float32)
    scale = lax.rsqrt(jnp.mean(wide * wide, axis=-1, keepdims=True) + epsilon)
    return (wide * scale * gain).astype(jnp.bfloat16)


def halves_of(table):
    high = table.astype(ml_dtypes.bfloat16)
    low = (table - high.astype(np.float64)).astype(ml_dtypes.bfloat16)
    return high, low


def transform_tables(rows, cols):
    size = rows * cols
    row = np.arange(rows, dtype=np.float64)
    col = np.arange(cols, dtype=np.float64)
    outer_angle = 2.0 * np.pi * (((row[:, None] + 0.25) * row[None, :]) % rows) / rows
    inner_angle = 2.0 * np.pi * ((col[:, None] * col[None, :]) % cols) / cols
    turn_angle = 2.0 * np.pi * (row[:, None] + 0.25) * col[None, :] / size
    outer = np.concatenate([np.cos(outer_angle), -np.sin(outer_angle)], axis=0)
    cos, sin = np.cos(inner_angle), np.sin(inner_angle)
    inner = np.block([[cos, -sin], [sin, cos]])
    outer_high, outer_low = halves_of(outer)
    inner_high, inner_low = halves_of(inner)
    back_high, back_low = halves_of(outer.T / size)
    products = [np.concatenate([outer_high, outer_low], axis=1)]
    products += [inner_high, inner_low, np.concatenate([back_high, back_low], axis=0)]
    turn = np.stack([np.cos(turn_angle), -np.sin(turn_angle)])
    return np.stack(products), turn.astype(np.float32)


def dot(left, right):
    return jnp.dot(left, right, preferred_element_type=jnp.float32)


def split(values):
    high = values.astype(jnp.bfloat16)
    return high, (values - high.astype(jnp.float32)).astype(jnp.bfloat16)


def dot_split(values, high_table, low_table):
    high, low = split(values)
    rows = values.shape[0]
    both = dot(jnp.concatenate([high, low], axis=0), high_table)
    return both[:rows] + both[rows:] + dot(high, low_table)


def delayed(values, by):
    rows, cols = values.shape
    turned = pltpu.roll(values, by, 1)
    above = pltpu.roll(turned, 1, 0)
    row = lax.broadcasted_iota(jnp.int32, (rows, cols), 0)
    col = lax.broadcasted_iota(jnp.int32, (rows, cols), 1)
    return jnp.where(col >= by, turned, jnp.where(row >= 1, above, 0.0))


def round_bf16(values):
    return values.astype(jnp.bfloat16).astype(jnp.float32)


def channel_kernel(mine, short_w, bias, u, products, turn, mixed):
    rows, cols = u.shape[1], u.shape[2]
    outer, inner_high, inner_low = products[0], products[1], products[2]
    back_high, back_low = products[3, :rows], products[3, rows:]
    turn_real, turn_imag = turn[0], turn[1]
    per_channel = jnp.concatenate([short_w[k] for k in range(short_w.shape[0])] + [bias[...]], axis=0)
    column = lax.broadcasted_iota(jnp.int32, per_channel.shape, 1)
    scalars = jnp.sum(jnp.where(column == mine[0], per_channel, 0.0), axis=1, keepdims=True)
    scalars = [scalars[k : k + 1] for k in range(scalars.shape[0])]

    def short(k):
        values = u[k].astype(jnp.float32)
        total = scalars[3 * k] * values
        total = total + scalars[3 * k + 1] * delayed(values, 1)
        total = total + scalars[3 * k + 2] * delayed(values, 2)
        return total.astype(jnp.bfloat16)

    def forward(signals):
        count = len(signals)
        side = jnp.concatenate(signals, axis=1) if count > 1 else signals[0]
        first = dot(outer, jnp.concatenate([side, side], axis=0))
        turned = []
        for k in range(count):
            real = first[:rows, k * cols : (k + 1) * cols]
            imag = first[rows:, k * cols : (k + 1) * cols]
            turned.append(
                jnp.concatenate(
                    [
                        real * turn_real - imag * turn_imag,
                        real * turn_imag + imag * turn_real,
                    ],
                    axis=1,
                )
            )
        stacked = jnp.concatenate(turned, axis=0) if count > 1 else turned[0]
        spectra = dot_split(stacked, inner_high, inner_low)
        return [
            (spectra[k * rows : (k + 1) * rows, :cols], spectra[k * rows : (k + 1) * rows, cols:])
            for k in range(count)
        ]

    def inverse(one, two):
        real = one[0] * two[0] - one[1] * two[1]
        negated = -one[0] * two[1] - one[1] * two[0]
        inner = dot_split(
            jnp.concatenate([real, negated], axis=1), inner_high, inner_low
        )
        real, negated = inner[:, :cols], inner[:, cols:]
        turned = jnp.concatenate(
            [
                real * turn_real - negated * turn_imag,
                -negated * turn_real - real * turn_imag,
            ],
            axis=0,
        )
        high, low = split(turned)
        side = dot(back_high, jnp.concatenate([high, low], axis=1))
        return side[:, :cols] + side[:, cols:] + dot(back_low, high)

    v = short(0)
    signal, response_one, response_two = forward([v, u[3], u[4]])
    first = inverse(signal, response_one) + scalars[9] * v.astype(jnp.float32)
    gated = (short(1).astype(jnp.float32) * round_bf16(first)).astype(jnp.bfloat16)
    (signal,) = forward([gated])
    second = inverse(signal, response_two) + scalars[10] * gated.astype(jnp.float32)
    mixed[...] = (short(2).astype(jnp.float32) * round_bf16(second)).astype(jnp.bfloat16)


def call(
    kernel, out_shape, flops, *operands, scalars=0, source=pltpu.VMEM, scratch=(), limit=16
):
    vmem = pl.BlockSpec(memory_space=pltpu.VMEM)
    smem = pl.BlockSpec(memory_space=pltpu.SMEM)
    held = pl.BlockSpec(memory_space=source)
    return pl.pallas_call(
        kernel,
        out_shape=out_shape,
        in_specs=[smem] * scalars + [held] * (len(operands) - scalars),
        out_specs=jax.tree.map(lambda _: vmem, out_shape),
        scratch_shapes=scratch,
        compiler_params=pltpu.CompilerParams(vmem_limit_bytes=limit * 2**20),
        cost_estimate=pl.CostEstimate(flops=flops, bytes_accessed=2**20, transcendentals=0),
    )(*operands)


def load_kernel(half, parity, *refs):
    count = (len(refs) - 2) // 2
    sources, (sent, *held), sems = refs[:count], refs[count:-1], refs[-1]
    w_up, w_out, w_down = sources[:3]
    units, wide = w_up.shape
    rows = w_out.shape[0]
    part = wide // 2
    there = pl.ds(pl.multiple_of((1 - half[0]) * part, part), part)
    here = pl.ds(pl.multiple_of(half[0] * part, part), part)
    turn = pl.ds(pl.multiple_of(parity[0] * part, part), part)
    pairs = [
        (w_up.at[:, turn], sent.at[pl.ds(0, units)]),
        (w_down.at[turn, there], sent.at[pl.ds(units, part)]),
        (w_out.at[:, pl.ds(0, part)], sent.at[pl.ds(units + part, rows)]),
        (w_out.at[:, pl.ds(part, part)], sent.at[pl.ds(units + part + rows, rows)]),
        (w_down.at[:, here], held[0]),
        (w_up, held[1]),
        (w_out, held[2]),
    ]
    pairs += list(zip(sources[3:], held[3:]))
    copies = [
        pltpu.make_async_copy(source, target, sems.at[k])
        for k, (source, target) in enumerate(pairs)
    ]
    for copy in copies:
        copy.start()
    for copy in copies:
        copy.wait()


def load(half, parity, w_up, w_out, w_down, *arrays):
    sources = [w_up, w_out, w_down, *arrays]
    sources = [pltpu.with_memory_space_constraint(array, pltpu.HBM) for array in sources]
    units, wide = w_up.shape
    part = wide // 2
    held = [
        pltpu.VMEM((units + part + 2 * w_out.shape[0], part), w_up.dtype),
        pltpu.VMEM((units, part), w_down.dtype),
    ]
    held += [pltpu.VMEM(array.shape, array.dtype) for array in (w_up, w_out, *arrays)]
    sems = [pltpu.SemaphoreType.DMA((len(sources) + 4,))]
    return call(
        load_kernel, held, 0, half, parity, *sources, source=pltpu.HBM, scratch=sems, scalars=2
    )


def project_kernel(whole, gain, w_in, filters, outgoing):
    normed = rms_norm(whole[...], gain[...])
    count = w_in.shape[0]
    for k in range(count):
        outgoing[k] = lax.dot_general(
            w_in[k], normed, (((0,), (1,)), ((), ())), preferred_element_type=jnp.float32
        ).astype(jnp.bfloat16)
    for k in range(filters.shape[0]):
        outgoing[count + k] = filters[k]


def out_kernel(half, arrived, own, near, partial):
    rows = arrived.shape[1]
    first = near.shape[0] - 2 * rows
    other = jnp.concatenate([near[first : first + rows], near[first + rows :]], axis=1)
    low = half[0] == 0
    weights = (jnp.where(low, own[...], other), jnp.where(low, other, own[...]))
    parts = [
        lax.dot_general(
            arrived[k], weights[k], (((0,), (0,)), ((), ())), preferred_element_type=jnp.float32
        )
        for k in range(2)
    ]
    partial[...] = parts[0] + parts[1]


def mlp_kernel(place, parity, whole, shares, gain, w_up, w_down, near, far, pieces, own):
    count, _, width = pieces.shape
    units = whole.shape[1]
    half_units = units // 2
    share = shares[0] + shares[1]
    middle = (whole[...].astype(jnp.float32) + share).astype(jnp.bfloat16)
    mine = middle[:, :width]
    for k in range(1, units // width):
        mine = jnp.where(place[0] == k, middle[:, k * width : (k + 1) * width], mine)
    own[...] = mine
    normed = rms_norm(middle, gain[...])
    hidden = jax.nn.gelu(dot(normed, w_up[...])).astype(jnp.bfloat16)
    partial = dot(hidden, w_down[...])
    for part in (near, far):
        hidden = jax.nn.gelu(dot(normed, part[:units])).astype(jnp.bfloat16)
        partial = partial + dot(hidden, part[units : units + half_units])
    partial = partial.astype(jnp.bfloat16)
    for k in range(count):
        pieces[k] = partial[:, k * width : (k + 1) * width]


def other_half_pairs():
    pairs = []
    for z in range(8):
        there = (z + 2) % 8
        if there // 4 == z // 4:
            there = (z - 2) % 8
        pairs.append((z % 4 * 2 + z // 4, there % 4 * 2 + there // 4))
    return pairs


def local(tokens, gain_mix, w_in, short_w, filters, conv_bias, w_out, gain_mlp, w_up, w_down):
    samples, width = tokens.shape
    shards = lax.axis_size(SEQ)
    blocks = lax.axis_size(CH)
    shape = jax.ShapeDtypeStruct
    mine = lax.axis_index(SEQ).astype(jnp.int32)[None]
    place = lax.axis_index(CH).astype(jnp.int32)[None]
    half = lax.axis_index("h").astype(jnp.int32)[None]
    parity = (lax.axis_index("x") % 2).astype(jnp.int32)[None]
    tables = [jnp.asarray(table) for table in transform_tables(shards, samples)]
    (
        sent,
        w_down,
        w_up,
        w_out,
        tokens,
        gain_mix,
        w_in,
        short_w,
        filters,
        conv_bias,
        gain_mlp,
        *tables,
    ) = load(
        half,
        parity,
        w_up,
        w_out,
        w_down,
        tokens,
        gain_mix[None],
        w_in,
        short_w,
        filters,
        conv_bias,
        gain_mlp[None],
        *tables,
    )
    whole = lax.all_gather(tokens, CH, axis=1, tiled=True)
    outgoing = call(
        project_kernel,
        shape((5, width, samples), jnp.bfloat16),
        2**26,
        whole,
        gain_mix,
        w_in,
        filters,
    )
    outgoing, sent, half, parity, place, mine = lax.optimization_barrier(
        (outgoing.transpose(1, 0, 2), sent, half, parity, place, mine)
    )
    arrived = lax.all_to_all(outgoing, SEQ, split_axis=0, concat_axis=0, tiled=True)
    near = lax.ppermute(sent, ("z", "h"), other_half_pairs())
    far = lax.ppermute(near[: width * blocks * 3 // 2], "x", [(k, k ^ 1) for k in range(lax.axis_size("x"))])
    mixed = call(
        channel_kernel,
        shape((shards, samples), jnp.bfloat16),
        2**29,
        mine,
        short_w,
        conv_bias,
        arrived.transpose(1, 0, 2),
        *tables,
        scalars=1,
    )
    doubled = jnp.concatenate([mixed, mixed], axis=0)
    returned = lax.all_to_all(doubled, ("h",) + SEQ, split_axis=0, concat_axis=0, tiled=True)
    partial = call(
        out_kernel,
        shape((samples, blocks * width), jnp.float32),
        2**31,
        half,
        returned.reshape(2, shards, samples),
        w_out,
        near,
        scalars=1,
    )
    shares = lax.all_gather(partial, "c", axis=0)
    pieces, own = call(
        mlp_kernel,
        (shape((2, samples, width), jnp.bfloat16), shape((samples, width), jnp.bfloat16)),
        2**28,
        place,
        parity,
        whole,
        shares,
        gain_mlp,
        w_up,
        w_down,
        near,
        far,
        scalars=2,
    )
    pieces = lax.all_gather(pieces, "c", axis=0)
    pieces = lax.dynamic_index_in_dim(pieces, place[0] % 2, 1, keepdims=False)
    total = jnp.sum(pieces.astype(jnp.float32), axis=0)
    return (own.astype(jnp.float32) + total).astype(jnp.bfloat16)


def solution(mesh):
    fine = Mesh(mesh.devices.reshape(4, 8, 4, 2, 2), SEQ + CH)
    return jax.shard_map(
        local,
        mesh=fine,
        in_specs=(
            P(SEQ, CH),
            P(),
            P(None, None, CH),
            P(None, None, CH),
            P(None, CH, SEQ),
            P(None, CH),
            P(CH, None),
            P(),
            P(None, CH),
            P(CH, None),
        ),
        out_specs=P(SEQ, CH),
        check_vma=False,
    )
```

```python
import jax
import jax.numpy as jnp
import ml_dtypes
import numpy as np
from jax import lax
from jax.experimental import pallas as pl
from jax.experimental.pallas import tpu as pltpu
from jax.sharding import Mesh, PartitionSpec as P

epsilon = 1e-06

SEQ = ("z", "y", "x")
CH = ("h", "c")
DEEP, HIGH, WIDE = 4, 8, 4


def rms_norm(values, gain):
    wide = values.astype(jnp.float32)
    scale = lax.rsqrt(jnp.mean(wide * wide, axis=-1, keepdims=True) + epsilon)
    return (wide * scale * gain).astype(jnp.bfloat16)


def halves_of(table):
    high = table.astype(ml_dtypes.bfloat16)
    low = (table - high.astype(np.float64)).astype(ml_dtypes.bfloat16)
    return high, low


def first_ranks(deep, high, wide):
    return [
        ((deep - 1 - z) * high + (y + high // 2) % high) * wide + (x + wide // 2) % wide
        for z in range(deep)
        for y in range(high)
        for x in range(wide)
    ]


def second_ranks(deep, high, wide):
    return [
        (((1 - h) * deep + z) * high + (y + high // 2) % high) * wide + (x + wide // 2) % wide
        for h in range(2)
        for z in range(deep)
        for y in range(high)
        for x in range(wide)
    ]


def previous_rows(times):
    times = np.asarray(times)
    return (times[:, None] == times[None, :] + 1).astype(ml_dtypes.bfloat16)


def transform_tables(rows, cols, times):
    size = rows * cols
    times = np.asarray(times)
    row = np.arange(rows, dtype=np.float64)
    col = np.arange(cols, dtype=np.float64)
    outer_angle = 2.0 * np.pi * (((row[:, None] + 0.25) * row[None, :]) % rows) / rows
    inner_angle = 2.0 * np.pi * ((col[:, None] * col[None, :]) % cols) / cols
    turn_angle = 2.0 * np.pi * (row[:, None] + 0.25) * col[None, :] / size
    outer = np.concatenate([np.cos(outer_angle), -np.sin(outer_angle)], axis=0)
    cos, sin = np.cos(inner_angle), np.sin(inner_angle)
    inner = np.block([[cos, -sin], [sin, cos]])
    outer = outer[:, times]
    outer_high, outer_low = halves_of(outer)
    inner_high, inner_low = halves_of(inner)
    back_high, back_low = halves_of(outer.T / size)
    products = [np.concatenate([outer_high, outer_low], axis=1)]
    products += [inner_high, inner_low, np.concatenate([back_high, back_low], axis=0)]
    turn = np.stack([np.cos(turn_angle), -np.sin(turn_angle)])
    return np.stack(products), turn.astype(np.float32)


def dot(left, right):
    return jnp.dot(left, right, preferred_element_type=jnp.float32)


def split(values):
    high = values.astype(jnp.bfloat16)
    return high, (values - high.astype(jnp.float32)).astype(jnp.bfloat16)


def dot_split(values, high_table, low_table):
    high, low = split(values)
    rows = values.shape[0]
    both = dot(jnp.concatenate([high, low], axis=0), high_table)
    return both[:rows] + both[rows:] + dot(high, low_table)


def delayed(values, above, by):
    col = lax.broadcasted_iota(jnp.int32, values.shape, 1)
    return jnp.where(col >= by, pltpu.roll(values, by, 1), pltpu.roll(above, by, 1))


def turned_blocks(values):
    step = values.shape[0] // DEEP
    return [values[k * step : (k + 1) * step] for k in reversed(range(DEEP))]


def round_bf16(values):
    return values.astype(jnp.bfloat16).astype(jnp.float32)


def channel_kernel(mine, short_w, bias, u, previous, products, turn, mixed):
    rows, cols = u.shape[1], u.shape[2]
    above = dot(previous[...], jnp.concatenate([u[0], u[1], u[2]], axis=1))
    outer, inner_high, inner_low = products[0], products[1], products[2]
    back_high, back_low = products[3, :rows], products[3, rows:]
    turn_real, turn_imag = turn[0], turn[1]
    per_channel = jnp.concatenate([short_w[k] for k in range(short_w.shape[0])] + [bias[...]], axis=0)
    column = lax.broadcasted_iota(jnp.int32, per_channel.shape, 1)
    scalars = jnp.sum(jnp.where(column == mine[0], per_channel, 0.0), axis=1, keepdims=True)
    scalars = [scalars[k : k + 1] for k in range(scalars.shape[0])]

    def short(k):
        values = u[k].astype(jnp.float32)
        total = scalars[3 * k] * values
        past = above[:, k * cols : (k + 1) * cols]
        total = total + scalars[3 * k + 1] * delayed(values, past, 1)
        total = total + scalars[3 * k + 2] * delayed(values, past, 2)
        return total.astype(jnp.bfloat16)

    def forward(signals):
        count = len(signals)
        side = jnp.concatenate(signals, axis=1) if count > 1 else signals[0]
        first = dot(outer, jnp.concatenate([side, side], axis=0))
        turned = []
        for k in range(count):
            real = first[:rows, k * cols : (k + 1) * cols]
            imag = first[rows:, k * cols : (k + 1) * cols]
            turned.append(
                jnp.concatenate(
                    [
                        real * turn_real - imag * turn_imag,
                        real * turn_imag + imag * turn_real,
                    ],
                    axis=1,
                )
            )
        stacked = jnp.concatenate(turned, axis=0) if count > 1 else turned[0]
        spectra = dot_split(stacked, inner_high, inner_low)
        return [
            (spectra[k * rows : (k + 1) * rows, :cols], spectra[k * rows : (k + 1) * rows, cols:])
            for k in range(count)
        ]

    def inverse(one, two):
        real = one[0] * two[0] - one[1] * two[1]
        negated = -one[0] * two[1] - one[1] * two[0]
        inner = dot_split(
            jnp.concatenate([real, negated], axis=1), inner_high, inner_low
        )
        real, negated = inner[:, :cols], inner[:, cols:]
        turned = jnp.concatenate(
            [
                real * turn_real - negated * turn_imag,
                -negated * turn_real - real * turn_imag,
            ],
            axis=0,
        )
        high, low = split(turned)
        side = dot(back_high, jnp.concatenate([high, low], axis=1))
        return side[:, :cols] + side[:, cols:] + dot(back_low, high)

    v = short(0)
    signal, response_one, response_two = forward([v, u[3], u[4]])
    first = inverse(signal, response_one) + scalars[9] * v.astype(jnp.float32)
    gated = (short(1).astype(jnp.float32) * round_bf16(first)).astype(jnp.bfloat16)
    (signal,) = forward([gated])
    second = inverse(signal, response_two) + scalars[10] * gated.astype(jnp.float32)
    product = (short(2).astype(jnp.float32) * round_bf16(second)).astype(jnp.bfloat16)
    mixed[...] = jnp.concatenate(turned_blocks(product), axis=0)


def call(
    kernel, out_shape, flops, *operands, scalars=0, source=pltpu.VMEM, scratch=(), limit=16
):
    vmem = pl.BlockSpec(memory_space=pltpu.VMEM)
    smem = pl.BlockSpec(memory_space=pltpu.SMEM)
    held = pl.BlockSpec(memory_space=source)
    return pl.pallas_call(
        kernel,
        out_shape=out_shape,
        in_specs=[smem] * scalars + [held] * (len(operands) - scalars),
        out_specs=jax.tree.map(lambda _: vmem, out_shape),
        scratch_shapes=scratch,
        compiler_params=pltpu.CompilerParams(vmem_limit_bytes=limit * 2**20),
        cost_estimate=pl.CostEstimate(flops=flops, bytes_accessed=2**20, transcendentals=0),
    )(*operands)


def copy_all(pairs, sems):
    copies = [
        pltpu.make_async_copy(source, target, sems.at[k])
        for k, (source, target) in enumerate(pairs)
    ]
    for copy in copies:
        copy.start()
    for copy in copies:
        copy.wait()


def first_load_kernel(half, parity, *refs):
    count = (len(refs) + 1) // 2
    sources, (sent, *held), sems = refs[:count], refs[count:-1], refs[-1]
    w_up, w_down, w_out = sources[:3]
    units, wide = w_up.shape
    rows = w_out.shape[0]
    part = wide // 2
    there = pl.ds(pl.multiple_of((1 - half[0]) * part, part), part)
    turn = pl.ds(pl.multiple_of(parity[0] * part, part), part)
    pairs = [
        (w_up.at[:, turn], sent.at[pl.ds(0, units)]),
        (w_down.at[turn, there], sent.at[pl.ds(units, part)]),
        (w_out.at[:, pl.ds(0, part)], sent.at[pl.ds(units + part, rows)]),
        (w_out.at[:, pl.ds(part, part)], sent.at[pl.ds(units + part + rows, rows)]),
    ]
    copy_all(pairs + list(zip(sources[3:], held)), sems)


def last_load_kernel(half, w_down, *refs):
    count = (len(refs) - 2) // 2
    sources, (down, *held), sems = refs[:count], refs[count:-1], refs[-1]
    part = down.shape[1]
    here = pl.ds(pl.multiple_of(half[0] * part, part), part)
    copy_all([(w_down.at[:, here], down)] + list(zip(sources, held)), sems)


def load(kernel, copies, cut, scalars, *arrays):
    arrays = [pltpu.with_memory_space_constraint(array, pltpu.HBM) for array in arrays]
    held = [pltpu.VMEM(cut, jnp.bfloat16)]
    held += [pltpu.VMEM(array.shape, array.dtype) for array in arrays[-(copies - 1) :]]
    sems = [pltpu.SemaphoreType.DMA((len(arrays) + 1,))]
    return call(
        kernel,
        held,
        0,
        *scalars,
        *arrays,
        scalars=len(scalars),
        source=pltpu.HBM,
        scratch=sems,
    )


def project_kernel(whole, gain, w_in, filters, outgoing):
    normed = rms_norm(whole[...], gain[...])
    count = w_in.shape[0]
    for k in range(count):
        outgoing[k] = lax.dot_general(
            w_in[k], normed, (((0,), (1,)), ((), ())), preferred_element_type=jnp.float32
        ).astype(jnp.bfloat16)
    for k in range(filters.shape[0]):
        outgoing[count + k] = filters[k]


def out_kernel(half, arrived, own, near, partial):
    rows = arrived.shape[1]
    first = near.shape[0] - 2 * rows
    other = jnp.concatenate([near[first : first + rows], near[first + rows :]], axis=1)
    low = half[0] == 0
    weights = (jnp.where(low, own[...], other), jnp.where(low, other, own[...]))
    parts = [
        lax.dot_general(
            jnp.concatenate(turned_blocks(arrived[1 - k]), axis=0),
            weights[k],
            (((0,), (0,)), ((), ())),
            preferred_element_type=jnp.float32,
        )
        for k in range(2)
    ]
    partial[...] = parts[0] + parts[1]


def mlp_kernel(place, parity, whole, shares, gain, w_up, w_down, near, far, pieces, own):
    count, _, width = pieces.shape
    units = whole.shape[1]
    half_units = units // 2
    share = shares[0] + shares[1]
    middle = (whole[...].astype(jnp.float32) + share).astype(jnp.bfloat16)
    mine = middle[:, :width]
    for k in range(1, units // width):
        mine = jnp.where(place[0] == k, middle[:, k * width : (k + 1) * width], mine)
    own[...] = mine
    normed = rms_norm(middle, gain[...])
    hidden = jax.nn.gelu(dot(normed, w_up[...])).astype(jnp.bfloat16)
    partial = dot(hidden, w_down[...])
    for part in (near, far):
        hidden = jax.nn.gelu(dot(normed, part[:units])).astype(jnp.bfloat16)
        partial = partial + dot(hidden, part[units : units + half_units])
    partial = partial.astype(jnp.bfloat16)
    for k in range(count):
        pieces[k] = partial[:, k * width : (k + 1) * width]


def other_half_pairs():
    pairs = []
    for z in range(8):
        there = (z + 2) % 8
        if there // 4 == z // 4:
            there = (z - 2) % 8
        pairs.append((z % 4 * 2 + z // 4, there % 4 * 2 + there // 4))
    return pairs


def neighbour_pairs():
    high, wide = lax.axis_size("y"), lax.axis_size("x")
    pairs = []
    for y in range(high):
        for x in range(wide):
            pairs.append(((y * wide + x) * 2, (y * wide + (x ^ 1)) * 2))
            pairs.append(((y * wide + x) * 2 + 1, ((y ^ 1) * wide + x) * 2 + 1))
    return pairs


def local(tokens, gain_mix, w_in, short_w, filters, conv_bias, w_out, gain_mlp, w_up, w_down):
    samples, width = tokens.shape
    shards = lax.axis_size(SEQ)
    blocks = lax.axis_size(CH)
    shape = jax.ShapeDtypeStruct
    place_z, place_y, place_x = (lax.axis_index(axis) for axis in SEQ)
    mine = (DEEP - 1 - place_z) * HIGH + (place_y + HIGH // 2) % HIGH
    mine = (mine * WIDE + (place_x + WIDE // 2) % WIDE).astype(jnp.int32)[None]
    ranks = first_ranks(DEEP, HIGH, WIDE)
    place = lax.axis_index(CH).astype(jnp.int32)[None]
    half = lax.axis_index("h").astype(jnp.int32)[None]
    side = jnp.where(lax.axis_index("c") == 0, lax.axis_index("x"), lax.axis_index("y"))
    parity = (side % 2).astype(jnp.int32)[None]
    tables = [previous_rows(ranks), *transform_tables(shards, samples, ranks)]
    tables = [jnp.asarray(table) for table in tables]
    units, wide = w_up.shape
    part = wide // 2
    sent, tokens, gain_mix, w_in, filters = load(
        first_load_kernel,
        5,
        (units + part + 2 * width, part),
        (half, parity),
        w_up,
        w_down,
        w_out,
        tokens,
        gain_mix[None],
        w_in,
        filters,
    )
    whole = lax.all_gather(tokens, CH, axis=1, tiled=True)
    outgoing = call(
        project_kernel,
        shape((5, width, samples), jnp.bfloat16),
        2**26,
        whole,
        gain_mix,
        w_in,
        filters,
    )
    outgoing, sent, half, parity, place, mine, w_up = lax.optimization_barrier(
        (outgoing.transpose(1, 0, 2), sent, half, parity, place, mine, w_up)
    )
    arrived = lax.all_to_all(
        outgoing, SEQ, split_axis=0, concat_axis=0, tiled=True, axis_index_groups=[ranks]
    )
    w_down, w_up, w_out, short_w, conv_bias, gain_mlp, *tables = load(
        last_load_kernel,
        9,
        (units, part),
        (half,),
        w_down,
        w_up,
        w_out,
        short_w,
        conv_bias,
        gain_mlp[None],
        *tables,
    )
    near = lax.ppermute(sent, ("z", "h"), other_half_pairs())
    far = lax.ppermute(near[: width * blocks * 3 // 2], ("y", "x", "c"), neighbour_pairs())
    mixed = call(
        channel_kernel,
        shape((shards, samples), jnp.bfloat16),
        2**29,
        mine,
        short_w,
        conv_bias,
        arrived.transpose(1, 0, 2),
        *tables,
        scalars=1,
    )
    doubled = jnp.concatenate([mixed, mixed], axis=0)
    returned = lax.all_to_all(
        doubled,
        ("h",) + SEQ,
        split_axis=0,
        concat_axis=0,
        tiled=True,
        axis_index_groups=[second_ranks(DEEP, HIGH, WIDE)],
    )
    partial = call(
        out_kernel,
        shape((samples, blocks * width), jnp.float32),
        2**31,
        half,
        returned.reshape(2, shards, samples),
        w_out,
        near,
        scalars=1,
    )
    shares = lax.all_gather(partial, "c", axis=0)
    pieces, own = call(
        mlp_kernel,
        (shape((2, samples, width), jnp.bfloat16), shape((samples, width), jnp.bfloat16)),
        2**28,
        place,
        parity,
        whole,
        shares,
        gain_mlp,
        w_up,
        w_down,
        near,
        far,
        scalars=2,
    )
    pieces = lax.all_gather(pieces, "c", axis=0)
    pieces = lax.dynamic_index_in_dim(pieces, place[0] % 2, 1, keepdims=False)
    total = jnp.sum(pieces.astype(jnp.float32), axis=0)
    return (own.astype(jnp.float32) + total).astype(jnp.bfloat16)


def solution(mesh):
    fine = Mesh(mesh.devices.reshape(4, 8, 4, 2, 2), SEQ + CH)
    return jax.shard_map(
        local,
        mesh=fine,
        in_specs=(
            P(SEQ, CH),
            P(),
            P(None, None, CH),
            P(None, None, CH),
            P(None, CH, SEQ),
            P(None, CH),
            P(CH, None),
            P(),
            P(None, CH),
            P(CH, None),
        ),
        out_specs=P(SEQ, CH),
        check_vma=False,
    )
```

```python
import jax
import jax.numpy as jnp
import ml_dtypes
import numpy as np
from jax import lax
from jax.experimental import pallas as pl
from jax.experimental.pallas import tpu as pltpu
from jax.sharding import Mesh, PartitionSpec as P

epsilon = 1e-06

SEQ = ("z", "y", "x")
CH = ("h", "c")
DEEP, HIGH, WIDE = 4, 8, 4


def rms_norm(values, gain):
    wide = values.astype(jnp.float32)
    scale = lax.rsqrt(jnp.mean(wide * wide, axis=-1, keepdims=True) + epsilon)
    return (wide * scale * gain).astype(jnp.bfloat16)


def halves_of(table):
    high = table.astype(ml_dtypes.bfloat16)
    low = (table - high.astype(np.float64)).astype(ml_dtypes.bfloat16)
    return high, low


def first_ranks(deep, high, wide):
    return [
        ((deep - 1 - z) * high + (y + high // 2) % high) * wide + (x + wide // 2) % wide
        for z in range(deep)
        for y in range(high)
        for x in range(wide)
    ]


def second_ranks(deep, high, wide):
    ranks = first_ranks(deep, high, wide)
    return [len(ranks) + rank for rank in ranks] + ranks


def previous_rows(times):
    times = np.asarray(times)
    return (times[:, None] == times[None, :] + 1).astype(ml_dtypes.bfloat16)


def transform_tables(rows, cols, times):
    size = rows * cols
    times = np.asarray(times)
    row = np.arange(rows, dtype=np.float64)
    col = np.arange(cols, dtype=np.float64)
    outer_angle = 2.0 * np.pi * (((row[:, None] + 0.25) * row[None, :]) % rows) / rows
    inner_angle = 2.0 * np.pi * ((col[:, None] * col[None, :]) % cols) / cols
    turn_angle = 2.0 * np.pi * (row[:, None] + 0.25) * col[None, :] / size
    outer = np.concatenate([np.cos(outer_angle), -np.sin(outer_angle)], axis=0)
    cos, sin = np.cos(inner_angle), np.sin(inner_angle)
    inner = np.block([[cos, -sin], [sin, cos]])
    outer = outer[:, times]
    outer_high, outer_low = halves_of(outer)
    inner_high, inner_low = halves_of(inner)
    back_high, back_low = halves_of(outer.T / size)
    products = [np.concatenate([outer_high, outer_low], axis=1)]
    products += [inner_high, inner_low, np.concatenate([back_high, back_low], axis=0)]
    turn = np.stack([np.cos(turn_angle), -np.sin(turn_angle)])
    return np.stack(products), turn.astype(np.float32)


def dot(left, right):
    return jnp.dot(left, right, preferred_element_type=jnp.float32)


def split(values):
    high = values.astype(jnp.bfloat16)
    return high, (values - high.astype(jnp.float32)).astype(jnp.bfloat16)


def dot_split(values, high_table, low_table):
    high, low = split(values)
    rows = values.shape[0]
    both = dot(jnp.concatenate([high, low], axis=0), high_table)
    return both[:rows] + both[rows:] + dot(high, low_table)


def delayed(values, above, by):
    col = lax.broadcasted_iota(jnp.int32, values.shape, 1)
    return jnp.where(col >= by, pltpu.roll(values, by, 1), pltpu.roll(above, by, 1))


def round_bf16(values):
    return values.astype(jnp.bfloat16).astype(jnp.float32)


def channel_kernel(mine, short_w, bias, u, previous, products, turn, mixed):
    rows, cols = u.shape[1], u.shape[2]
    above = dot(previous[...], jnp.concatenate([u[0], u[1], u[2]], axis=1))
    outer, inner_high, inner_low = products[0], products[1], products[2]
    back_high, back_low = products[3, :rows], products[3, rows:]
    turn_real, turn_imag = turn[0], turn[1]
    per_channel = jnp.concatenate([short_w[k] for k in range(short_w.shape[0])] + [bias[...]], axis=0)
    column = lax.broadcasted_iota(jnp.int32, per_channel.shape, 1)
    scalars = jnp.sum(jnp.where(column == mine[0], per_channel, 0.0), axis=1, keepdims=True)
    scalars = [scalars[k : k + 1] for k in range(scalars.shape[0])]

    def short(k):
        values = u[k].astype(jnp.float32)
        total = scalars[3 * k] * values
        past = above[:, k * cols : (k + 1) * cols]
        total = total + scalars[3 * k + 1] * delayed(values, past, 1)
        total = total + scalars[3 * k + 2] * delayed(values, past, 2)
        return total.astype(jnp.bfloat16)

    def forward(signals):
        count = len(signals)
        side = jnp.concatenate(signals, axis=1) if count > 1 else signals[0]
        first = dot(outer, jnp.concatenate([side, side], axis=0))
        turned = []
        for k in range(count):
            real = first[:rows, k * cols : (k + 1) * cols]
            imag = first[rows:, k * cols : (k + 1) * cols]
            turned.append(
                jnp.concatenate(
                    [
                        real * turn_real - imag * turn_imag,
                        real * turn_imag + imag * turn_real,
                    ],
                    axis=1,
                )
            )
        stacked = jnp.concatenate(turned, axis=0) if count > 1 else turned[0]
        spectra = dot_split(stacked, inner_high, inner_low)
        return [
            (spectra[k * rows : (k + 1) * rows, :cols], spectra[k * rows : (k + 1) * rows, cols:])
            for k in range(count)
        ]

    def inverse(one, two):
        real = one[0] * two[0] - one[1] * two[1]
        negated = -one[0] * two[1] - one[1] * two[0]
        inner = dot_split(
            jnp.concatenate([real, negated], axis=1), inner_high, inner_low
        )
        real, negated = inner[:, :cols], inner[:, cols:]
        turned = jnp.concatenate(
            [
                real * turn_real - negated * turn_imag,
                -negated * turn_real - real * turn_imag,
            ],
            axis=0,
        )
        high, low = split(turned)
        side = dot(back_high, jnp.concatenate([high, low], axis=1))
        return side[:, :cols] + side[:, cols:] + dot(back_low, high)

    v = short(0)
    signal, response_one, response_two = forward([v, u[3], u[4]])
    first = inverse(signal, response_one) + scalars[9] * v.astype(jnp.float32)
    gated = (short(1).astype(jnp.float32) * round_bf16(first)).astype(jnp.bfloat16)
    (signal,) = forward([gated])
    second = inverse(signal, response_two) + scalars[10] * gated.astype(jnp.float32)
    mixed[...] = (short(2).astype(jnp.float32) * round_bf16(second)).astype(jnp.bfloat16)


def call(
    kernel, out_shape, flops, *operands, scalars=0, source=pltpu.VMEM, scratch=(), limit=16
):
    vmem = pl.BlockSpec(memory_space=pltpu.VMEM)
    smem = pl.BlockSpec(memory_space=pltpu.SMEM)
    held = pl.BlockSpec(memory_space=source)
    return pl.pallas_call(
        kernel,
        out_shape=out_shape,
        in_specs=[smem] * scalars + [held] * (len(operands) - scalars),
        out_specs=jax.tree.map(lambda _: vmem, out_shape),
        scratch_shapes=scratch,
        compiler_params=pltpu.CompilerParams(vmem_limit_bytes=limit * 2**20),
        cost_estimate=pl.CostEstimate(flops=flops, bytes_accessed=2**20, transcendentals=0),
    )(*operands)


def copy_all(pairs, sems):
    copies = [
        pltpu.make_async_copy(source, target, sems.at[k])
        for k, (source, target) in enumerate(pairs)
    ]
    for copy in copies:
        copy.start()
    for copy in copies:
        copy.wait()


def first_load_kernel(half, parity, *refs):
    count = (len(refs) + 1) // 2
    sources, (sent, *held), sems = refs[:count], refs[count:-1], refs[-1]
    w_up, w_down, w_out = sources[:3]
    units, wide = w_up.shape
    rows = w_out.shape[0]
    part = wide // 2
    there = pl.ds(pl.multiple_of((1 - half[0]) * part, part), part)
    turn = pl.ds(pl.multiple_of(parity[0] * part, part), part)
    pairs = [
        (w_up.at[:, turn], sent.at[pl.ds(0, units)]),
        (w_down.at[turn, there], sent.at[pl.ds(units, part)]),
        (w_out.at[:, pl.ds(0, part)], sent.at[pl.ds(units + part, rows)]),
        (w_out.at[:, pl.ds(part, part)], sent.at[pl.ds(units + part + rows, rows)]),
    ]
    copy_all(pairs + list(zip(sources[3:], held)), sems)


def last_load_kernel(half, w_down, *refs):
    count = (len(refs) - 2) // 2
    sources, (down, *held), sems = refs[:count], refs[count:-1], refs[-1]
    part = down.shape[1]
    here = pl.ds(pl.multiple_of(half[0] * part, part), part)
    copy_all([(w_down.at[:, here], down)] + list(zip(sources, held)), sems)


def load(kernel, copies, cut, scalars, *arrays):
    arrays = [pltpu.with_memory_space_constraint(array, pltpu.HBM) for array in arrays]
    held = [pltpu.VMEM(cut, jnp.bfloat16)]
    held += [pltpu.VMEM(array.shape, array.dtype) for array in arrays[-(copies - 1) :]]
    sems = [pltpu.SemaphoreType.DMA((len(arrays) + 1,))]
    return call(
        kernel,
        held,
        0,
        *scalars,
        *arrays,
        scalars=len(scalars),
        source=pltpu.HBM,
        scratch=sems,
    )


def project_kernel(whole, gain, w_in, filters, outgoing):
    normed = rms_norm(whole[...], gain[...])
    count = w_in.shape[0]
    for k in range(count):
        outgoing[k] = lax.dot_general(
            w_in[k], normed, (((0,), (1,)), ((), ())), preferred_element_type=jnp.float32
        ).astype(jnp.bfloat16)
    for k in range(filters.shape[0]):
        outgoing[count + k] = filters[k]


def out_kernel(half, arrived, own, near, partial):
    rows = arrived.shape[1]
    first = near.shape[0] - 2 * rows
    other = jnp.concatenate([near[first : first + rows], near[first + rows :]], axis=1)
    low = half[0] == 0
    weights = (jnp.where(low, own[...], other), jnp.where(low, other, own[...]))
    parts = [
        lax.dot_general(
            arrived[1 - k],
            weights[k],
            (((0,), (0,)), ((), ())),
            preferred_element_type=jnp.float32,
        )
        for k in range(2)
    ]
    partial[...] = parts[0] + parts[1]


def mlp_kernel(place, whole, shares, gain, w_up, w_down, near, own, normed, partial):
    units = whole.shape[1]
    width = own.shape[1]
    half_units = units // 2
    share = shares[0] + shares[1]
    middle = (whole[...].astype(jnp.float32) + share).astype(jnp.bfloat16)
    mine = middle[:, :width]
    for k in range(1, units // width):
        mine = jnp.where(place[0] == k, middle[:, k * width : (k + 1) * width], mine)
    own[...] = mine
    scaled = rms_norm(middle, gain[...])
    normed[...] = scaled
    hidden = jax.nn.gelu(dot(scaled, w_up[...])).astype(jnp.bfloat16)
    total = dot(hidden, w_down[...])
    hidden = jax.nn.gelu(dot(scaled, near[:units])).astype(jnp.bfloat16)
    partial[...] = total + dot(hidden, near[units : units + half_units])


def far_kernel(normed, partial, far, pieces):
    count, _, width = pieces.shape
    units = normed.shape[1]
    hidden = jax.nn.gelu(dot(normed[...], far[:units])).astype(jnp.bfloat16)
    total = (partial[...] + dot(hidden, far[units:])).astype(jnp.bfloat16)
    for k in range(count):
        pieces[k] = total[:, k * width : (k + 1) * width]


def other_half_pairs():
    pairs = []
    for z in range(8):
        there = (z + 2) % 8
        if there // 4 == z // 4:
            there = (z - 2) % 8
        pairs.append((z % 4 * 2 + z // 4, there % 4 * 2 + there // 4))
    return pairs


def neighbour_pairs():
    high, wide = lax.axis_size("y"), lax.axis_size("x")
    pairs = []
    for y in range(high):
        for x in range(wide):
            pairs.append(((y * wide + x) * 2, (y * wide + (x ^ 1)) * 2))
            pairs.append(((y * wide + x) * 2 + 1, ((y ^ 1) * wide + x) * 2 + 1))
    return pairs


def local(tokens, gain_mix, w_in, short_w, filters, conv_bias, w_out, gain_mlp, w_up, w_down):
    samples, width = tokens.shape
    shards = lax.axis_size(SEQ)
    blocks = lax.axis_size(CH)
    shape = jax.ShapeDtypeStruct
    place_z, place_y, place_x = (lax.axis_index(axis) for axis in SEQ)
    mine = (DEEP - 1 - place_z) * HIGH + (place_y + HIGH // 2) % HIGH
    mine = (mine * WIDE + (place_x + WIDE // 2) % WIDE).astype(jnp.int32)[None]
    ranks = first_ranks(DEEP, HIGH, WIDE)
    place = lax.axis_index(CH).astype(jnp.int32)[None]
    half = lax.axis_index("h").astype(jnp.int32)[None]
    side = jnp.where(lax.axis_index("c") == 0, lax.axis_index("x"), lax.axis_index("y"))
    parity = (side % 2).astype(jnp.int32)[None]
    tables = [previous_rows(ranks), *transform_tables(shards, samples, ranks)]
    tables = [jnp.asarray(table) for table in tables]
    units, wide = w_up.shape
    part = wide // 2
    sent, tokens, gain_mix, w_in, filters = load(
        first_load_kernel,
        5,
        (units + part + 2 * width, part),
        (half, parity),
        w_up,
        w_down,
        w_out,
        tokens,
        gain_mix[None],
        w_in,
        filters,
    )
    whole = lax.all_gather(tokens, CH, axis=1, tiled=True)
    outgoing = call(
        project_kernel,
        shape((5, width, samples), jnp.bfloat16),
        2**26,
        whole,
        gain_mix,
        w_in,
        filters,
    )
    outgoing, sent, half, parity, place, mine, w_up = lax.optimization_barrier(
        (outgoing.transpose(1, 0, 2), sent, half, parity, place, mine, w_up)
    )
    arrived = lax.all_to_all(
        outgoing, SEQ, split_axis=0, concat_axis=0, tiled=True, axis_index_groups=[ranks]
    )
    w_down, w_up, w_out, short_w, conv_bias, gain_mlp, *tables = load(
        last_load_kernel,
        9,
        (units, part),
        (half,),
        w_down,
        w_up,
        w_out,
        short_w,
        conv_bias,
        gain_mlp[None],
        *tables,
    )
    near = lax.ppermute(sent, ("z", "h"), other_half_pairs())
    far = lax.ppermute(near[: width * blocks * 3 // 2], ("y", "x", "c"), neighbour_pairs())
    mixed = call(
        channel_kernel,
        shape((shards, samples), jnp.bfloat16),
        2**29,
        mine,
        short_w,
        conv_bias,
        arrived.transpose(1, 0, 2),
        *tables,
        scalars=1,
    )
    doubled = jnp.concatenate([mixed, mixed], axis=0)
    returned = lax.all_to_all(
        doubled,
        ("h",) + SEQ,
        split_axis=0,
        concat_axis=0,
        tiled=True,
        axis_index_groups=[second_ranks(DEEP, HIGH, WIDE)],
    )
    partial = call(
        out_kernel,
        shape((samples, blocks * width), jnp.float32),
        2**31,
        half,
        returned.reshape(2, shards, samples),
        w_out,
        near,
        scalars=1,
    )
    shares = lax.all_gather(partial, "c", axis=0)
    own, normed, partial = call(
        mlp_kernel,
        (
            shape((samples, width), jnp.bfloat16),
            shape((samples, blocks * width), jnp.bfloat16),
            shape((samples, part), jnp.float32),
        ),
        2**28,
        place,
        whole,
        shares,
        gain_mlp,
        w_up,
        w_down,
        near,
        scalars=1,
    )
    pieces = call(
        far_kernel, shape((2, samples, width), jnp.bfloat16), 2**27, normed, partial, far
    )
    pieces = lax.all_gather(pieces, "c", axis=0)
    pieces = lax.dynamic_index_in_dim(pieces, place[0] % 2, 1, keepdims=False)
    total = jnp.sum(pieces.astype(jnp.float32), axis=0)
    return (own.astype(jnp.float32) + total).astype(jnp.bfloat16)


def solution(mesh):
    fine = Mesh(mesh.devices.reshape(4, 8, 4, 2, 2), SEQ + CH)
    return jax.shard_map(
        local,
        mesh=fine,
        in_specs=(
            P(SEQ, CH),
            P(),
            P(None, None, CH),
            P(None, None, CH),
            P(None, CH, SEQ),
            P(None, CH),
            P(CH, None),
            P(),
            P(None, CH),
            P(CH, None),
        ),
        out_specs=P(SEQ, CH),
        check_vma=False,
    )
```

```python
import jax
import jax.numpy as jnp
import ml_dtypes
import numpy as np
from jax import lax
from jax.experimental import pallas as pl
from jax.experimental.pallas import tpu as pltpu
from jax.sharding import Mesh, PartitionSpec as P

epsilon = 1e-06

SEQ = ("z", "y", "x")
CH = ("h", "c")
DEEP, HIGH, WIDE = 4, 8, 4


def rms_norm(values, gain):
    wide = values.astype(jnp.float32)
    scale = lax.rsqrt(jnp.mean(wide * wide, axis=-1, keepdims=True) + epsilon)
    return (wide * scale * gain).astype(jnp.bfloat16)


def halves_of(table):
    high = table.astype(ml_dtypes.bfloat16)
    low = (table - high.astype(np.float64)).astype(ml_dtypes.bfloat16)
    return high, low


def first_ranks(deep, high, wide):
    return [
        ((deep - 1 - z) * high + (y + high // 2) % high) * wide + (x + wide - 1) % wide
        for z in range(deep)
        for y in range(high)
        for x in range(wide)
    ]


def second_ranks(deep, high, wide):
    ranks = first_ranks(deep, high, wide)
    return [len(ranks) + rank for rank in ranks] + ranks


def previous_rows(times):
    times = np.asarray(times)
    return (times[:, None] == times[None, :] + 1).astype(ml_dtypes.bfloat16)


def transform_tables(rows, cols, times):
    size = rows * cols
    times = np.asarray(times)
    row = np.arange(rows, dtype=np.float64)
    col = np.arange(cols, dtype=np.float64)
    outer_angle = 2.0 * np.pi * (((row[:, None] + 0.25) * row[None, :]) % rows) / rows
    inner_angle = 2.0 * np.pi * ((col[:, None] * col[None, :]) % cols) / cols
    turn_angle = 2.0 * np.pi * (row[:, None] + 0.25) * col[None, :] / size
    outer = np.concatenate([np.cos(outer_angle), -np.sin(outer_angle)], axis=0)
    cos, sin = np.cos(inner_angle), np.sin(inner_angle)
    inner = np.block([[cos, -sin], [sin, cos]])
    outer = outer[:, times]
    outer_high, outer_low = halves_of(outer)
    inner_high, inner_low = halves_of(inner)
    back_high, back_low = halves_of(outer.T / size)
    products = [np.concatenate([outer_high, outer_low], axis=1)]
    products += [inner_high, inner_low, np.concatenate([back_high, back_low], axis=0)]
    turn = np.stack([np.cos(turn_angle), -np.sin(turn_angle)])
    return np.stack(products), turn.astype(np.float32)


def dot(left, right):
    return jnp.dot(left, right, preferred_element_type=jnp.float32)


def split(values):
    high = values.astype(jnp.bfloat16)
    return high, (values - high.astype(jnp.float32)).astype(jnp.bfloat16)


def dot_split(values, high_table, low_table):
    high, low = split(values)
    rows = values.shape[0]
    both = dot(jnp.concatenate([high, low], axis=0), high_table)
    return both[:rows] + both[rows:] + dot(high, low_table)


def delayed(values, above, by):
    col = lax.broadcasted_iota(jnp.int32, values.shape, 1)
    return jnp.where(col >= by, pltpu.roll(values, by, 1), pltpu.roll(above, by, 1))


def round_bf16(values):
    return values.astype(jnp.bfloat16).astype(jnp.float32)


def channel_kernel(mine, short_w, bias, u, previous, products, turn, mixed):
    rows, cols = u.shape[1], u.shape[2] // 3
    projected = u[0]
    above = dot(previous[...], projected)
    outer, inner_high, inner_low = products[0], products[1], products[2]
    back_high, back_low = products[3, :rows], products[3, rows:]
    turn_real, turn_imag = turn[0], turn[1]
    per_channel = jnp.concatenate([short_w[k] for k in range(short_w.shape[0])] + [bias[...]], axis=0)
    column = lax.broadcasted_iota(jnp.int32, per_channel.shape, 1)
    scalars = jnp.sum(jnp.where(column == mine[0], per_channel, 0.0), axis=1, keepdims=True)
    scalars = [scalars[k : k + 1] for k in range(scalars.shape[0])]

    def short(k):
        values = projected[:, k * cols : (k + 1) * cols].astype(jnp.float32)
        total = scalars[3 * k] * values
        past = above[:, k * cols : (k + 1) * cols]
        total = total + scalars[3 * k + 1] * delayed(values, past, 1)
        total = total + scalars[3 * k + 2] * delayed(values, past, 2)
        return total.astype(jnp.bfloat16)

    def forward(signals):
        count = len(signals)
        side = jnp.concatenate(signals, axis=1) if count > 1 else signals[0]
        first = dot(outer, jnp.concatenate([side, side], axis=0))
        turned = []
        for k in range(count):
            real = first[:rows, k * cols : (k + 1) * cols]
            imag = first[rows:, k * cols : (k + 1) * cols]
            turned.append(
                jnp.concatenate(
                    [
                        real * turn_real - imag * turn_imag,
                        real * turn_imag + imag * turn_real,
                    ],
                    axis=1,
                )
            )
        stacked = jnp.concatenate(turned, axis=0) if count > 1 else turned[0]
        spectra = dot_split(stacked, inner_high, inner_low)
        return [
            (spectra[k * rows : (k + 1) * rows, :cols], spectra[k * rows : (k + 1) * rows, cols:])
            for k in range(count)
        ]

    def inverse(one, two):
        real = one[0] * two[0] - one[1] * two[1]
        negated = -one[0] * two[1] - one[1] * two[0]
        inner = dot_split(
            jnp.concatenate([real, negated], axis=1), inner_high, inner_low
        )
        real, negated = inner[:, :cols], inner[:, cols:]
        turned = jnp.concatenate(
            [
                real * turn_real - negated * turn_imag,
                -negated * turn_real - real * turn_imag,
            ],
            axis=0,
        )
        high, low = split(turned)
        side = dot(back_high, jnp.concatenate([high, low], axis=1))
        return side[:, :cols] + side[:, cols:] + dot(back_low, high)

    v = short(0)
    signal, response_one, response_two = forward([v, u[1, :, :cols], u[1, :, cols : 2 * cols]])
    first = inverse(signal, response_one) + scalars[9] * v.astype(jnp.float32)
    gated = (short(1).astype(jnp.float32) * round_bf16(first)).astype(jnp.bfloat16)
    (signal,) = forward([gated])
    second = inverse(signal, response_two) + scalars[10] * gated.astype(jnp.float32)
    mixed[...] = (short(2).astype(jnp.float32) * round_bf16(second)).astype(jnp.bfloat16)


def call(
    kernel, out_shape, flops, *operands, scalars=0, source=pltpu.VMEM, scratch=(), limit=16
):
    vmem = pl.BlockSpec(memory_space=pltpu.VMEM)
    smem = pl.BlockSpec(memory_space=pltpu.SMEM)
    held = pl.BlockSpec(memory_space=source)
    return pl.pallas_call(
        kernel,
        out_shape=out_shape,
        in_specs=[smem] * scalars + [held] * (len(operands) - scalars),
        out_specs=jax.tree.map(lambda _: vmem, out_shape),
        scratch_shapes=scratch,
        compiler_params=pltpu.CompilerParams(vmem_limit_bytes=limit * 2**20),
        cost_estimate=pl.CostEstimate(flops=flops, bytes_accessed=2**20, transcendentals=0),
    )(*operands)


def copy_all(pairs, sems):
    copies = [
        pltpu.make_async_copy(source, target, sems.at[k])
        for k, (source, target) in enumerate(pairs)
    ]
    for copy in copies:
        copy.start()
    for copy in copies:
        copy.wait()


def first_load_kernel(half, parity, *refs):
    count = (len(refs) + 1) // 2
    sources, (sent, *held), sems = refs[:count], refs[count:-1], refs[-1]
    w_up, w_down, w_out = sources[:3]
    units, wide = w_up.shape
    rows = w_out.shape[0]
    part = wide // 2
    there = pl.ds(pl.multiple_of((1 - half[0]) * part, part), part)
    turn = pl.ds(pl.multiple_of(parity[0] * part, part), part)
    pairs = [
        (w_up.at[:, turn], sent.at[pl.ds(0, units)]),
        (w_down.at[turn, there], sent.at[pl.ds(units, part)]),
        (w_out.at[:, pl.ds(0, part)], sent.at[pl.ds(units + part, rows)]),
        (w_out.at[:, pl.ds(part, part)], sent.at[pl.ds(units + part + rows, rows)]),
    ]
    copy_all(pairs + list(zip(sources[3:], held)), sems)


def last_load_kernel(half, w_down, *refs):
    count = (len(refs) - 2) // 2
    sources, (down, *held), sems = refs[:count], refs[count:-1], refs[-1]
    part = down.shape[1]
    here = pl.ds(pl.multiple_of(half[0] * part, part), part)
    copy_all([(w_down.at[:, here], down)] + list(zip(sources, held)), sems)


def load(kernel, copies, cut, scalars, *arrays):
    arrays = [pltpu.with_memory_space_constraint(array, pltpu.HBM) for array in arrays]
    held = [pltpu.VMEM(cut, jnp.bfloat16)]
    held += [pltpu.VMEM(array.shape, array.dtype) for array in arrays[-(copies - 1) :]]
    sems = [pltpu.SemaphoreType.DMA((len(arrays) + 1,))]
    return call(
        kernel,
        held,
        0,
        *scalars,
        *arrays,
        scalars=len(scalars),
        source=pltpu.HBM,
        scratch=sems,
    )


def project_kernel(whole, gain, w_in, filters, outgoing):
    normed = rms_norm(whole[...], gain[...])
    count, _, width = w_in.shape
    for k in range(count):
        outgoing[0, :, k * width : (k + 1) * width] = lax.dot_general(
            w_in[k], normed, (((0,), (1,)), ((), ())), preferred_element_type=jnp.float32
        ).astype(jnp.bfloat16)
    outgoing[1] = jnp.concatenate([filters[0], filters[1], jnp.zeros_like(filters[0])], axis=1)


def out_kernel(half, arrived, own, near, partial):
    rows = arrived.shape[1]
    first = near.shape[0] - 2 * rows
    other = jnp.concatenate([near[first : first + rows], near[first + rows :]], axis=1)
    low = half[0] == 0
    weights = (jnp.where(low, own[...], other), jnp.where(low, other, own[...]))
    parts = [
        lax.dot_general(
            arrived[1 - k],
            weights[k],
            (((0,), (0,)), ((), ())),
            preferred_element_type=jnp.float32,
        )
        for k in range(2)
    ]
    partial[...] = parts[0] + parts[1]


def mlp_kernel(place, whole, shares, gain, w_up, w_down, near, own, normed, partial):
    units = whole.shape[1]
    width = own.shape[1]
    half_units = units // 2
    share = shares[0] + shares[1]
    middle = (whole[...].astype(jnp.float32) + share).astype(jnp.bfloat16)
    mine = middle[:, :width]
    for k in range(1, units // width):
        mine = jnp.where(place[0] == k, middle[:, k * width : (k + 1) * width], mine)
    own[...] = mine
    scaled = rms_norm(middle, gain[...])
    normed[...] = scaled
    hidden = jax.nn.gelu(dot(scaled, w_up[...])).astype(jnp.bfloat16)
    total = dot(hidden, w_down[...])
    hidden = jax.nn.gelu(dot(scaled, near[:units])).astype(jnp.bfloat16)
    partial[...] = total + dot(hidden, near[units : units + half_units])


def far_kernel(normed, partial, far, pieces):
    count, _, width = pieces.shape
    units = normed.shape[1]
    hidden = jax.nn.gelu(dot(normed[...], far[:units])).astype(jnp.bfloat16)
    total = (partial[...] + dot(hidden, far[units:])).astype(jnp.bfloat16)
    for k in range(count):
        pieces[k] = total[:, k * width : (k + 1) * width]


def other_half_pairs():
    pairs = []
    for z in range(8):
        there = (z + 2) % 8
        if there // 4 == z // 4:
            there = (z - 2) % 8
        pairs.append((z % 4 * 2 + z // 4, there % 4 * 2 + there // 4))
    return pairs


def neighbour_pairs():
    high, wide = lax.axis_size("y"), lax.axis_size("x")
    pairs = []
    for y in range(high):
        for x in range(wide):
            pairs.append(((y * wide + x) * 2, ((y ^ 1) * wide + x) * 2))
            pairs.append(((y * wide + x) * 2 + 1, (y * wide + (x ^ 1)) * 2 + 1))
    return pairs


def local(tokens, gain_mix, w_in, short_w, filters, conv_bias, w_out, gain_mlp, w_up, w_down):
    samples, width = tokens.shape
    shards = lax.axis_size(SEQ)
    blocks = lax.axis_size(CH)
    shape = jax.ShapeDtypeStruct
    place_z, place_y, place_x = (lax.axis_index(axis) for axis in SEQ)
    mine = (DEEP - 1 - place_z) * HIGH + (place_y + HIGH // 2) % HIGH
    mine = (mine * WIDE + (place_x + 1) % WIDE).astype(jnp.int32)[None]
    ranks = first_ranks(DEEP, HIGH, WIDE)
    place = lax.axis_index(CH).astype(jnp.int32)[None]
    half = lax.axis_index("h").astype(jnp.int32)[None]
    side = jnp.where(lax.axis_index("c") == 0, lax.axis_index("y"), lax.axis_index("x"))
    parity = (side % 2).astype(jnp.int32)[None]
    tables = [previous_rows(ranks), *transform_tables(shards, samples, ranks)]
    tables = [jnp.asarray(table) for table in tables]
    units, wide = w_up.shape
    part = wide // 2
    sent, tokens, gain_mix, w_in, filters = load(
        first_load_kernel,
        5,
        (units + part + 2 * width, part),
        (half, parity),
        w_up,
        w_down,
        w_out,
        tokens,
        gain_mix[None],
        w_in,
        filters,
    )
    whole = lax.all_gather(tokens, CH, axis=1, tiled=True)
    outgoing = call(
        project_kernel,
        shape((2, width, 3 * samples), jnp.bfloat16),
        2**26,
        whole,
        gain_mix,
        w_in,
        filters,
    )
    outgoing, sent, half, parity, place, mine, w_up = lax.optimization_barrier(
        (outgoing.transpose(1, 0, 2), sent, half, parity, place, mine, w_up)
    )
    arrived = lax.all_to_all(
        outgoing, SEQ, split_axis=0, concat_axis=0, tiled=True, axis_index_groups=[ranks]
    )
    w_down, w_up, w_out, short_w, conv_bias, gain_mlp, *tables = load(
        last_load_kernel,
        9,
        (units, part),
        (half,),
        w_down,
        w_up,
        w_out,
        short_w,
        conv_bias,
        gain_mlp[None],
        *tables,
    )
    near = lax.ppermute(sent, ("z", "h"), other_half_pairs())
    far = lax.ppermute(near[: width * blocks * 3 // 2], ("y", "x", "c"), neighbour_pairs())
    mixed = call(
        channel_kernel,
        shape((shards, samples), jnp.bfloat16),
        2**29,
        mine,
        short_w,
        conv_bias,
        arrived.transpose(1, 0, 2),
        *tables,
        scalars=1,
    )
    doubled = jnp.concatenate([mixed, mixed], axis=0)
    returned = lax.all_to_all(
        doubled,
        ("h",) + SEQ,
        split_axis=0,
        concat_axis=0,
        tiled=True,
        axis_index_groups=[second_ranks(DEEP, HIGH, WIDE)],
    )
    partial = call(
        out_kernel,
        shape((samples, blocks * width), jnp.float32),
        2**31,
        half,
        returned.reshape(2, shards, samples),
        w_out,
        near,
        scalars=1,
    )
    shares = lax.all_gather(partial, "c", axis=0)
    own, normed, partial = call(
        mlp_kernel,
        (
            shape((samples, width), jnp.bfloat16),
            shape((samples, blocks * width), jnp.bfloat16),
            shape((samples, part), jnp.float32),
        ),
        2**28,
        place,
        whole,
        shares,
        gain_mlp,
        w_up,
        w_down,
        near,
        scalars=1,
    )
    pieces = call(
        far_kernel, shape((2, samples, width), jnp.bfloat16), 2**27, normed, partial, far
    )
    pieces = lax.all_gather(pieces, "c", axis=0)
    pieces = lax.dynamic_index_in_dim(pieces, place[0] % 2, 1, keepdims=False)
    total = jnp.sum(pieces.astype(jnp.float32), axis=0)
    return (own.astype(jnp.float32) + total).astype(jnp.bfloat16)


def solution(mesh):
    fine = Mesh(mesh.devices.reshape(4, 8, 4, 2, 2), SEQ + CH)
    return jax.shard_map(
        local,
        mesh=fine,
        in_specs=(
            P(SEQ, CH),
            P(),
            P(None, None, CH),
            P(None, None, CH),
            P(None, CH, SEQ),
            P(None, CH),
            P(CH, None),
            P(),
            P(None, CH),
            P(CH, None),
        ),
        out_specs=P(SEQ, CH),
        check_vma=False,
    )
```

```python
import jax
import jax.numpy as jnp
import ml_dtypes
import numpy as np
from jax import lax
from jax.experimental import pallas as pl
from jax.experimental.pallas import tpu as pltpu
from jax.sharding import Mesh, PartitionSpec as P

epsilon = 1e-06

SEQ = ("z", "y", "x")
CH = ("h", "c")
DEEP, HIGH, WIDE = 4, 8, 4


def rms_norm(values, gain):
    wide = values.astype(jnp.float32)
    scale = lax.rsqrt(jnp.mean(wide * wide, axis=-1, keepdims=True) + epsilon)
    return (wide * scale * gain).astype(jnp.bfloat16)


def halves_of(table):
    high = table.astype(ml_dtypes.bfloat16)
    low = (table - high.astype(np.float64)).astype(ml_dtypes.bfloat16)
    return high, low


def first_ranks(deep, high, wide):
    return [
        ((deep - 1 - z) * high + (y + high // 2) % high) * wide + (x + wide - 1) % wide
        for z in range(deep)
        for y in range(high)
        for x in range(wide)
    ]


def second_ranks(deep, high, wide):
    ranks = first_ranks(deep, high, wide)
    return [len(ranks) + rank for rank in ranks] + ranks


def previous_rows(times):
    times = np.asarray(times)
    return (times[:, None] == times[None, :] + 1).astype(ml_dtypes.bfloat16)


def transform_tables(rows, cols, times):
    size = rows * cols
    times = np.asarray(times)
    row = np.arange(rows, dtype=np.float64)
    col = np.arange(cols, dtype=np.float64)
    outer_angle = 2.0 * np.pi * (((row[:, None] + 0.25) * row[None, :]) % rows) / rows
    inner_angle = 2.0 * np.pi * ((col[:, None] * col[None, :]) % cols) / cols
    turn_angle = 2.0 * np.pi * (row[:, None] + 0.25) * col[None, :] / size
    outer = np.concatenate([np.cos(outer_angle), -np.sin(outer_angle)], axis=0)
    cos, sin = np.cos(inner_angle), np.sin(inner_angle)
    inner = np.block([[cos, -sin], [sin, cos]])
    outer = outer[:, times]
    outer_high, outer_low = halves_of(outer)
    inner_high, inner_low = halves_of(inner)
    back_high, back_low = halves_of(outer.T / size)
    products = [np.concatenate([outer_high, outer_low], axis=1)]
    products += [inner_high, inner_low, np.concatenate([back_high, back_low], axis=0)]
    turn = np.stack([np.cos(turn_angle), -np.sin(turn_angle)])
    return np.stack(products), turn.astype(np.float32)


def dot(left, right):
    return jnp.dot(left, right, preferred_element_type=jnp.float32)


def split(values):
    high = values.astype(jnp.bfloat16)
    return high, (values - high.astype(jnp.float32)).astype(jnp.bfloat16)


def dot_split(values, high_table, low_table):
    high, low = split(values)
    rows = values.shape[0]
    both = dot(jnp.concatenate([high, low], axis=0), high_table)
    return both[:rows] + both[rows:] + dot(high, low_table)


def delayed(values, above, by):
    col = lax.broadcasted_iota(jnp.int32, values.shape, 1)
    return jnp.where(col >= by, pltpu.roll(values, by, 1), pltpu.roll(above, by, 1))


def round_bf16(values):
    return values.astype(jnp.bfloat16).astype(jnp.float32)


def channel_kernel(mine, short_w, bias, u, previous, products, turn, mixed):
    rows, cols = u.shape[1], u.shape[2] // 3
    projected = u[0]
    above = dot(previous[...], projected)
    outer, inner_high, inner_low = products[0], products[1], products[2]
    back_high, back_low = products[3, :rows], products[3, rows:]
    turn_real, turn_imag = turn[0], turn[1]
    per_channel = jnp.concatenate([short_w[k] for k in range(short_w.shape[0])] + [bias[...]], axis=0)
    column = lax.broadcasted_iota(jnp.int32, per_channel.shape, 1)
    scalars = jnp.sum(jnp.where(column == mine[0], per_channel, 0.0), axis=1, keepdims=True)
    scalars = [scalars[k : k + 1] for k in range(scalars.shape[0])]

    def short(k):
        values = projected[:, k * cols : (k + 1) * cols].astype(jnp.float32)
        total = scalars[3 * k] * values
        past = above[:, k * cols : (k + 1) * cols]
        total = total + scalars[3 * k + 1] * delayed(values, past, 1)
        total = total + scalars[3 * k + 2] * delayed(values, past, 2)
        return total.astype(jnp.bfloat16)

    def forward(signals):
        count = len(signals)
        side = jnp.concatenate(signals, axis=1) if count > 1 else signals[0]
        first = dot(outer, jnp.concatenate([side, side], axis=0))
        turned = []
        for k in range(count):
            real = first[:rows, k * cols : (k + 1) * cols]
            imag = first[rows:, k * cols : (k + 1) * cols]
            turned.append(
                jnp.concatenate(
                    [
                        real * turn_real - imag * turn_imag,
                        real * turn_imag + imag * turn_real,
                    ],
                    axis=1,
                )
            )
        stacked = jnp.concatenate(turned, axis=0) if count > 1 else turned[0]
        spectra = dot_split(stacked, inner_high, inner_low)
        return [
            (spectra[k * rows : (k + 1) * rows, :cols], spectra[k * rows : (k + 1) * rows, cols:])
            for k in range(count)
        ]

    def inverse(one, two):
        real = one[0] * two[0] - one[1] * two[1]
        negated = -one[0] * two[1] - one[1] * two[0]
        inner = dot_split(
            jnp.concatenate([real, negated], axis=1), inner_high, inner_low
        )
        real, negated = inner[:, :cols], inner[:, cols:]
        turned = jnp.concatenate(
            [
                real * turn_real - negated * turn_imag,
                -negated * turn_real - real * turn_imag,
            ],
            axis=0,
        )
        high, low = split(turned)
        side = dot(back_high, jnp.concatenate([high, low], axis=1))
        return side[:, :cols] + side[:, cols:] + dot(back_low, high)

    v = short(0)
    (response_one,) = forward([u[1, :, :cols]])
    (response_two,) = forward([u[1, :, cols : 2 * cols]])
    (signal,) = forward([v])
    first = inverse(signal, response_one) + scalars[9] * v.astype(jnp.float32)
    gated = (short(1).astype(jnp.float32) * round_bf16(first)).astype(jnp.bfloat16)
    (signal,) = forward([gated])
    second = inverse(signal, response_two) + scalars[10] * gated.astype(jnp.float32)
    mixed[...] = (short(2).astype(jnp.float32) * round_bf16(second)).astype(jnp.bfloat16)


def call(
    kernel, out_shape, flops, *operands, scalars=0, source=pltpu.VMEM, scratch=(), limit=16
):
    vmem = pl.BlockSpec(memory_space=pltpu.VMEM)
    smem = pl.BlockSpec(memory_space=pltpu.SMEM)
    held = pl.BlockSpec(memory_space=source)
    return pl.pallas_call(
        kernel,
        out_shape=out_shape,
        in_specs=[smem] * scalars + [held] * (len(operands) - scalars),
        out_specs=jax.tree.map(lambda _: vmem, out_shape),
        scratch_shapes=scratch,
        compiler_params=pltpu.CompilerParams(vmem_limit_bytes=limit * 2**20),
        cost_estimate=pl.CostEstimate(flops=flops, bytes_accessed=2**20, transcendentals=0),
    )(*operands)


def copy_all(pairs, sems):
    copies = [
        pltpu.make_async_copy(source, target, sems.at[k])
        for k, (source, target) in enumerate(pairs)
    ]
    for copy in copies:
        copy.start()
    for copy in copies:
        copy.wait()


def first_load_kernel(half, parity, *refs):
    count = (len(refs) + 1) // 2
    sources, (sent, *held), sems = refs[:count], refs[count:-1], refs[-1]
    w_up, w_down, w_out = sources[:3]
    units, wide = w_up.shape
    rows = w_out.shape[0]
    part = wide // 2
    there = pl.ds(pl.multiple_of((1 - half[0]) * part, part), part)
    turn = pl.ds(pl.multiple_of(parity[0] * part, part), part)
    pairs = [
        (w_up.at[:, turn], sent.at[pl.ds(0, units)]),
        (w_down.at[turn, there], sent.at[pl.ds(units, part)]),
        (w_out.at[:, pl.ds(0, part)], sent.at[pl.ds(units + part, rows)]),
        (w_out.at[:, pl.ds(part, part)], sent.at[pl.ds(units + part + rows, rows)]),
    ]
    copy_all(pairs + list(zip(sources[3:], held)), sems)


def last_load_kernel(half, w_down, *refs):
    count = (len(refs) - 2) // 2
    sources, (down, *held), sems = refs[:count], refs[count:-1], refs[-1]
    part = down.shape[1]
    here = pl.ds(pl.multiple_of(half[0] * part, part), part)
    copy_all([(w_down.at[:, here], down)] + list(zip(sources, held)), sems)


def load(kernel, copies, cut, scalars, *arrays):
    arrays = [pltpu.with_memory_space_constraint(array, pltpu.HBM) for array in arrays]
    held = [pltpu.VMEM(cut, jnp.bfloat16)]
    held += [pltpu.VMEM(array.shape, array.dtype) for array in arrays[-(copies - 1) :]]
    sems = [pltpu.SemaphoreType.DMA((len(arrays) + 1,))]
    return call(
        kernel,
        held,
        0,
        *scalars,
        *arrays,
        scalars=len(scalars),
        source=pltpu.HBM,
        scratch=sems,
    )


def project_kernel(whole, gain, w_in, filters, outgoing):
    normed = rms_norm(whole[...], gain[...])
    count, _, width = w_in.shape
    for k in range(count):
        outgoing[0, :, k * width : (k + 1) * width] = lax.dot_general(
            w_in[k], normed, (((0,), (1,)), ((), ())), preferred_element_type=jnp.float32
        ).astype(jnp.bfloat16)
    outgoing[1] = jnp.concatenate([filters[0], filters[1], jnp.zeros_like(filters[0])], axis=1)


def out_kernel(half, arrived, own, near, partial):
    rows = arrived.shape[1]
    first = near.shape[0] - 2 * rows
    other = jnp.concatenate([near[first : first + rows], near[first + rows :]], axis=1)
    low = half[0] == 0
    weights = (jnp.where(low, own[...], other), jnp.where(low, other, own[...]))
    parts = [
        lax.dot_general(
            arrived[1 - k],
            weights[k],
            (((0,), (0,)), ((), ())),
            preferred_element_type=jnp.float32,
        )
        for k in range(2)
    ]
    partial[...] = parts[0] + parts[1]


def mlp_kernel(place, whole, shares, gain, w_up, w_down, near, own, normed, partial):
    units = whole.shape[1]
    width = own.shape[1]
    half_units = units // 2
    share = shares[0] + shares[1]
    middle = (whole[...].astype(jnp.float32) + share).astype(jnp.bfloat16)
    mine = middle[:, :width]
    for k in range(1, units // width):
        mine = jnp.where(place[0] == k, middle[:, k * width : (k + 1) * width], mine)
    own[...] = mine
    scaled = rms_norm(middle, gain[...])
    normed[...] = scaled
    hidden = jax.nn.gelu(dot(scaled, w_up[...])).astype(jnp.bfloat16)
    total = dot(hidden, w_down[...])
    hidden = jax.nn.gelu(dot(scaled, near[:units])).astype(jnp.bfloat16)
    partial[...] = total + dot(hidden, near[units : units + half_units])


def far_kernel(normed, partial, far, pieces):
    count, _, width = pieces.shape
    units = normed.shape[1]
    hidden = jax.nn.gelu(dot(normed[...], far[:units])).astype(jnp.bfloat16)
    total = (partial[...] + dot(hidden, far[units:])).astype(jnp.bfloat16)
    for k in range(count):
        pieces[k] = total[:, k * width : (k + 1) * width]


def other_half_pairs():
    pairs = []
    for z in range(8):
        there = (z + 2) % 8
        if there // 4 == z // 4:
            there = (z - 2) % 8
        pairs.append((z % 4 * 2 + z // 4, there % 4 * 2 + there // 4))
    return pairs


def neighbour_pairs():
    high, wide = lax.axis_size("y"), lax.axis_size("x")
    pairs = []
    for y in range(high):
        for x in range(wide):
            pairs.append(((y * wide + x) * 2, ((y ^ 1) * wide + x) * 2))
            pairs.append(((y * wide + x) * 2 + 1, (y * wide + (x ^ 1)) * 2 + 1))
    return pairs


def local(tokens, gain_mix, w_in, short_w, filters, conv_bias, w_out, gain_mlp, w_up, w_down):
    samples, width = tokens.shape
    shards = lax.axis_size(SEQ)
    blocks = lax.axis_size(CH)
    shape = jax.ShapeDtypeStruct
    place_z, place_y, place_x = (lax.axis_index(axis) for axis in SEQ)
    mine = (DEEP - 1 - place_z) * HIGH + (place_y + HIGH // 2) % HIGH
    mine = (mine * WIDE + (place_x + 1) % WIDE).astype(jnp.int32)[None]
    ranks = first_ranks(DEEP, HIGH, WIDE)
    place = lax.axis_index(CH).astype(jnp.int32)[None]
    half = lax.axis_index("h").astype(jnp.int32)[None]
    side = jnp.where(lax.axis_index("c") == 0, lax.axis_index("y"), lax.axis_index("x"))
    parity = (side % 2).astype(jnp.int32)[None]
    tables = [previous_rows(ranks), *transform_tables(shards, samples, ranks)]
    tables = [jnp.asarray(table) for table in tables]
    units, wide = w_up.shape
    part = wide // 2
    sent, tokens, gain_mix, w_in, filters = load(
        first_load_kernel,
        5,
        (units + part + 2 * width, part),
        (half, parity),
        w_up,
        w_down,
        w_out,
        tokens,
        gain_mix[None],
        w_in,
        filters,
    )
    whole = lax.all_gather(tokens, CH, axis=1, tiled=True)
    outgoing = call(
        project_kernel,
        shape((2, width, 3 * samples), jnp.bfloat16),
        2**26,
        whole,
        gain_mix,
        w_in,
        filters,
    )
    outgoing, sent, half, parity, place, mine, w_up = lax.optimization_barrier(
        (outgoing.transpose(1, 0, 2), sent, half, parity, place, mine, w_up)
    )
    arrived = lax.all_to_all(
        outgoing, SEQ, split_axis=0, concat_axis=0, tiled=True, axis_index_groups=[ranks]
    )
    w_down, w_up, w_out, short_w, conv_bias, gain_mlp, *tables = load(
        last_load_kernel,
        9,
        (units, part),
        (half,),
        w_down,
        w_up,
        w_out,
        short_w,
        conv_bias,
        gain_mlp[None],
        *tables,
    )
    near = lax.ppermute(sent, ("z", "h"), other_half_pairs())
    far = lax.ppermute(near[: width * blocks * 3 // 2], ("y", "x", "c"), neighbour_pairs())
    mixed = call(
        channel_kernel,
        shape((shards, samples), jnp.bfloat16),
        2**29,
        mine,
        short_w,
        conv_bias,
        arrived.transpose(1, 0, 2),
        *tables,
        scalars=1,
    )
    doubled = jnp.concatenate([mixed, mixed], axis=0)
    returned = lax.all_to_all(
        doubled,
        ("h",) + SEQ,
        split_axis=0,
        concat_axis=0,
        tiled=True,
        axis_index_groups=[second_ranks(DEEP, HIGH, WIDE)],
    )
    partial = call(
        out_kernel,
        shape((samples, blocks * width), jnp.float32),
        2**31,
        half,
        returned.reshape(2, shards, samples),
        w_out,
        near,
        scalars=1,
    )
    shares = lax.all_gather(partial, "c", axis=0)
    own, normed, partial = call(
        mlp_kernel,
        (
            shape((samples, width), jnp.bfloat16),
            shape((samples, blocks * width), jnp.bfloat16),
            shape((samples, part), jnp.float32),
        ),
        2**28,
        place,
        whole,
        shares,
        gain_mlp,
        w_up,
        w_down,
        near,
        scalars=1,
    )
    pieces = call(
        far_kernel, shape((2, samples, width), jnp.bfloat16), 2**27, normed, partial, far
    )
    pieces = lax.all_gather(pieces, "c", axis=0)
    pieces = lax.dynamic_index_in_dim(pieces, place[0] % 2, 1, keepdims=False)
    total = jnp.sum(pieces.astype(jnp.float32), axis=0)
    return (own.astype(jnp.float32) + total).astype(jnp.bfloat16)


def solution(mesh):
    fine = Mesh(mesh.devices.reshape(4, 8, 4, 2, 2), SEQ + CH)
    return jax.shard_map(
        local,
        mesh=fine,
        in_specs=(
            P(SEQ, CH),
            P(),
            P(None, None, CH),
            P(None, None, CH),
            P(None, CH, SEQ),
            P(None, CH),
            P(CH, None),
            P(),
            P(None, CH),
            P(CH, None),
        ),
        out_specs=P(SEQ, CH),
        check_vma=False,
    )
```

```python
import jax
import jax.numpy as jnp
import ml_dtypes
import numpy as np
from jax import lax
from jax.experimental import pallas as pl
from jax.experimental.pallas import tpu as pltpu
from jax.sharding import Mesh, PartitionSpec as P

epsilon = 1e-06

SEQ = ("z", "y", "x")
CH = ("h", "c")
DEEP, HIGH, WIDE = 4, 8, 4


def rms_norm(values, gain):
    wide = values.astype(jnp.float32)
    scale = lax.rsqrt(jnp.mean(wide * wide, axis=-1, keepdims=True) + epsilon)
    return (wide * scale * gain).astype(jnp.bfloat16)


def halves_of(table):
    high = table.astype(ml_dtypes.bfloat16)
    low = (table - high.astype(np.float64)).astype(ml_dtypes.bfloat16)
    return high, low


def first_ranks(deep, high, wide):
    return [
        ((deep - 1 - z) * high + (y + high // 2) % high) * wide + (x + wide - 1) % wide
        for z in range(deep)
        for y in range(high)
        for x in range(wide)
    ]


def second_ranks(deep, high, wide):
    ranks = first_ranks(deep, high, wide)
    return [len(ranks) + rank for rank in ranks] + ranks


def previous_rows(times):
    times = np.asarray(times)
    return (times[:, None] == times[None, :] + 1).astype(ml_dtypes.bfloat16)


def transform_tables(rows, cols, times):
    size = rows * cols
    times = np.asarray(times)
    row = np.arange(rows, dtype=np.float64)
    col = np.arange(cols, dtype=np.float64)
    outer_angle = 2.0 * np.pi * (((row[:, None] + 0.25) * row[None, :]) % rows) / rows
    inner_angle = 2.0 * np.pi * ((col[:, None] * col[None, :]) % cols) / cols
    turn_angle = 2.0 * np.pi * (row[:, None] + 0.25) * col[None, :] / size
    outer = np.concatenate([np.cos(outer_angle), -np.sin(outer_angle)], axis=0)
    cos, sin = np.cos(inner_angle), np.sin(inner_angle)
    inner = np.block([[cos, -sin], [sin, cos]])
    outer = outer[:, times]
    outer_high, outer_low = halves_of(outer)
    inner_high, inner_low = halves_of(inner)
    back_high, back_low = halves_of(outer.T / size)
    products = [np.concatenate([outer_high, outer_low], axis=1)]
    products += [inner_high, inner_low, np.concatenate([back_high, back_low], axis=0)]
    turn = np.stack([np.cos(turn_angle), -np.sin(turn_angle)])
    return np.stack(products), turn.astype(np.float32)


def dot(left, right):
    return jnp.dot(left, right, preferred_element_type=jnp.float32)


def split(values):
    high = values.astype(jnp.bfloat16)
    return high, (values - high.astype(jnp.float32)).astype(jnp.bfloat16)


def dot_split(values, high_table, low_table):
    high, low = split(values)
    rows = values.shape[0]
    both = dot(jnp.concatenate([high, low], axis=0), high_table)
    return both[:rows] + both[rows:] + dot(high, low_table)


def delayed(values, above, by):
    col = lax.broadcasted_iota(jnp.int32, values.shape, 1)
    return jnp.where(col >= by, pltpu.roll(values, by, 1), pltpu.roll(above, by, 1))


def round_bf16(values):
    return values.astype(jnp.bfloat16).astype(jnp.float32)


def channel_kernel(mine, short_w, bias, u, previous, products, turn, mixed):
    rows, cols = u.shape[1], u.shape[2] // 3
    projected = u[0]
    above = dot(previous[...], projected)
    outer, inner_high, inner_low = products[0], products[1], products[2]
    back_high, back_low = products[3, :rows], products[3, rows:]
    turn_real, turn_imag = turn[0], turn[1]
    per_channel = jnp.concatenate([short_w[k] for k in range(short_w.shape[0])] + [bias[...]], axis=0)
    column = lax.broadcasted_iota(jnp.int32, per_channel.shape, 1)
    scalars = jnp.sum(jnp.where(column == mine[0], per_channel, 0.0), axis=1, keepdims=True)
    scalars = [scalars[k : k + 1] for k in range(scalars.shape[0])]

    def short(k):
        values = projected[:, k * cols : (k + 1) * cols].astype(jnp.float32)
        total = scalars[3 * k] * values
        past = above[:, k * cols : (k + 1) * cols]
        total = total + scalars[3 * k + 1] * delayed(values, past, 1)
        total = total + scalars[3 * k + 2] * delayed(values, past, 2)
        return total.astype(jnp.bfloat16)

    def forward(signals):
        count = len(signals)
        side = jnp.concatenate(signals, axis=1) if count > 1 else signals[0]
        first = dot(outer, jnp.concatenate([side, side], axis=0))
        turned = []
        for k in range(count):
            real = first[:rows, k * cols : (k + 1) * cols]
            imag = first[rows:, k * cols : (k + 1) * cols]
            turned.append(
                jnp.concatenate(
                    [
                        real * turn_real - imag * turn_imag,
                        real * turn_imag + imag * turn_real,
                    ],
                    axis=1,
                )
            )
        stacked = jnp.concatenate(turned, axis=0) if count > 1 else turned[0]
        spectra = dot_split(stacked, inner_high, inner_low)
        return [
            (spectra[k * rows : (k + 1) * rows, :cols], spectra[k * rows : (k + 1) * rows, cols:])
            for k in range(count)
        ]

    def inverse(one, two):
        real = one[0] * two[0] - one[1] * two[1]
        negated = -one[0] * two[1] - one[1] * two[0]
        inner = dot_split(
            jnp.concatenate([real, negated], axis=1), inner_high, inner_low
        )
        real, negated = inner[:, :cols], inner[:, cols:]
        turned = jnp.concatenate(
            [
                real * turn_real - negated * turn_imag,
                -negated * turn_real - real * turn_imag,
            ],
            axis=0,
        )
        high, low = split(turned)
        side = dot(back_high, jnp.concatenate([high, low], axis=1))
        return side[:, :cols] + side[:, cols:] + dot(back_low, high)

    v = short(0)
    (response_one,) = forward([u[1, :, :cols]])
    (response_two,) = forward([u[1, :, cols : 2 * cols]])
    (signal,) = forward([v])
    first = inverse(signal, response_one) + scalars[9] * v.astype(jnp.float32)
    gated = (short(1).astype(jnp.float32) * round_bf16(first)).astype(jnp.bfloat16)
    (signal,) = forward([gated])
    second = inverse(signal, response_two) + scalars[10] * gated.astype(jnp.float32)
    mixed[...] = (short(2).astype(jnp.float32) * round_bf16(second)).astype(jnp.bfloat16)


def call(
    kernel, out_shape, flops, *operands, scalars=0, source=pltpu.VMEM, scratch=(), limit=16
):
    vmem = pl.BlockSpec(memory_space=pltpu.VMEM)
    smem = pl.BlockSpec(memory_space=pltpu.SMEM)
    held = pl.BlockSpec(memory_space=source)
    return pl.pallas_call(
        kernel,
        out_shape=out_shape,
        in_specs=[smem] * scalars + [held] * (len(operands) - scalars),
        out_specs=jax.tree.map(lambda _: vmem, out_shape),
        scratch_shapes=scratch,
        compiler_params=pltpu.CompilerParams(vmem_limit_bytes=limit * 2**20),
        cost_estimate=pl.CostEstimate(flops=flops, bytes_accessed=2**20, transcendentals=0),
    )(*operands)


def copy_all(pairs, sems):
    copies = [
        pltpu.make_async_copy(source, target, sems.at[k])
        for k, (source, target) in enumerate(pairs)
    ]
    for copy in copies:
        copy.start()
    for copy in copies:
        copy.wait()


def first_load_kernel(half, parity, *refs):
    count = (len(refs) + 1) // 2
    sources, (sent, *held), sems = refs[:count], refs[count:-1], refs[-1]
    w_up, w_down, w_out = sources[:3]
    units, wide = w_up.shape
    rows = w_out.shape[0]
    part = wide // 2
    there = pl.ds(pl.multiple_of((1 - half[0]) * part, part), part)
    turn = pl.ds(pl.multiple_of(parity[0] * part, part), part)
    pairs = [
        (w_up.at[:, turn], sent.at[pl.ds(0, units)]),
        (w_down.at[turn, there], sent.at[pl.ds(units, part)]),
        (w_out.at[:, pl.ds(0, part)], sent.at[pl.ds(units + part, rows)]),
        (w_out.at[:, pl.ds(part, part)], sent.at[pl.ds(units + part + rows, rows)]),
    ]
    copy_all(pairs + list(zip(sources[3:], held)), sems)


def last_load_kernel(half, w_down, *refs):
    count = (len(refs) - 2) // 2
    sources, (down, *held), sems = refs[:count], refs[count:-1], refs[-1]
    part = down.shape[1]
    here = pl.ds(pl.multiple_of(half[0] * part, part), part)
    copy_all([(w_down.at[:, here], down)] + list(zip(sources, held)), sems)


def load(kernel, copies, cut, scalars, *arrays):
    arrays = [pltpu.with_memory_space_constraint(array, pltpu.HBM) for array in arrays]
    held = [pltpu.VMEM(cut, jnp.bfloat16)]
    held += [pltpu.VMEM(array.shape, array.dtype) for array in arrays[-(copies - 1) :]]
    sems = [pltpu.SemaphoreType.DMA((len(arrays) + 1,))]
    return call(
        kernel,
        held,
        0,
        *scalars,
        *arrays,
        scalars=len(scalars),
        source=pltpu.HBM,
        scratch=sems,
    )


def project_kernel(whole, gain, w_in, filters, outgoing):
    normed = rms_norm(whole[...], gain[...])
    count, _, width = w_in.shape
    for k in range(count):
        outgoing[0, :, k * width : (k + 1) * width] = lax.dot_general(
            w_in[k], normed, (((0,), (1,)), ((), ())), preferred_element_type=jnp.float32
        ).astype(jnp.bfloat16)
    outgoing[1] = jnp.concatenate([filters[0], filters[1], jnp.zeros_like(filters[0])], axis=1)


def out_kernel(half, arrived, own, near, partial):
    rows = arrived.shape[1]
    first = near.shape[0] - 2 * rows
    other = jnp.concatenate([near[first : first + rows], near[first + rows :]], axis=1)
    low = half[0] == 0
    weights = (jnp.where(low, own[...], other), jnp.where(low, other, own[...]))
    parts = [
        lax.dot_general(
            arrived[1 - k],
            weights[k],
            (((0,), (0,)), ((), ())),
            preferred_element_type=jnp.float32,
        )
        for k in range(2)
    ]
    partial[...] = (parts[0] + parts[1]).astype(partial.dtype)


def mlp_kernel(place, whole, shares, gain, w_up, w_down, near, own, normed, partial):
    units = whole.shape[1]
    width = own.shape[1]
    half_units = units // 2
    share = shares[0].astype(jnp.float32) + shares[1].astype(jnp.float32)
    middle = (whole[...].astype(jnp.float32) + share).astype(jnp.bfloat16)
    mine = middle[:, :width]
    for k in range(1, units // width):
        mine = jnp.where(place[0] == k, middle[:, k * width : (k + 1) * width], mine)
    own[...] = mine
    scaled = rms_norm(middle, gain[...])
    normed[...] = scaled
    hidden = jax.nn.gelu(dot(scaled, w_up[...])).astype(jnp.bfloat16)
    total = dot(hidden, w_down[...])
    hidden = jax.nn.gelu(dot(scaled, near[:units])).astype(jnp.bfloat16)
    partial[...] = total + dot(hidden, near[units : units + half_units])


def far_kernel(normed, partial, far, pieces):
    count, _, width = pieces.shape
    units = normed.shape[1]
    hidden = jax.nn.gelu(dot(normed[...], far[:units])).astype(jnp.bfloat16)
    total = (partial[...] + dot(hidden, far[units:])).astype(jnp.bfloat16)
    for k in range(count):
        pieces[k] = total[:, k * width : (k + 1) * width]


def other_half_pairs():
    pairs = []
    for z in range(8):
        there = (z + 2) % 8
        if there // 4 == z // 4:
            there = (z - 2) % 8
        pairs.append((z % 4 * 2 + z // 4, there % 4 * 2 + there // 4))
    return pairs


def neighbour_pairs():
    high, wide = lax.axis_size("y"), lax.axis_size("x")
    pairs = []
    for y in range(high):
        for x in range(wide):
            pairs.append(((y * wide + x) * 2, ((y ^ 1) * wide + x) * 2))
            pairs.append(((y * wide + x) * 2 + 1, (y * wide + (x ^ 1)) * 2 + 1))
    return pairs


def local(tokens, gain_mix, w_in, short_w, filters, conv_bias, w_out, gain_mlp, w_up, w_down):
    samples, width = tokens.shape
    shards = lax.axis_size(SEQ)
    blocks = lax.axis_size(CH)
    shape = jax.ShapeDtypeStruct
    place_z, place_y, place_x = (lax.axis_index(axis) for axis in SEQ)
    mine = (DEEP - 1 - place_z) * HIGH + (place_y + HIGH // 2) % HIGH
    mine = (mine * WIDE + (place_x + 1) % WIDE).astype(jnp.int32)[None]
    ranks = first_ranks(DEEP, HIGH, WIDE)
    place = lax.axis_index(CH).astype(jnp.int32)[None]
    half = lax.axis_index("h").astype(jnp.int32)[None]
    side = jnp.where(lax.axis_index("c") == 0, lax.axis_index("y"), lax.axis_index("x"))
    parity = (side % 2).astype(jnp.int32)[None]
    tables = [previous_rows(ranks), *transform_tables(shards, samples, ranks)]
    tables = [jnp.asarray(table) for table in tables]
    units, wide = w_up.shape
    part = wide // 2
    sent, tokens, gain_mix, w_in, filters = load(
        first_load_kernel,
        5,
        (units + part + 2 * width, part),
        (half, parity),
        w_up,
        w_down,
        w_out,
        tokens,
        gain_mix[None],
        w_in,
        filters,
    )
    whole = lax.all_gather(tokens, CH, axis=1, tiled=True)
    outgoing = call(
        project_kernel,
        shape((2, width, 3 * samples), jnp.bfloat16),
        2**26,
        whole,
        gain_mix,
        w_in,
        filters,
    )
    outgoing, sent, half, parity, place, mine, w_up = lax.optimization_barrier(
        (outgoing.transpose(1, 0, 2), sent, half, parity, place, mine, w_up)
    )
    arrived = lax.all_to_all(
        outgoing, SEQ, split_axis=0, concat_axis=0, tiled=True, axis_index_groups=[ranks]
    )
    w_down, w_up, w_out, short_w, conv_bias, gain_mlp, *tables = load(
        last_load_kernel,
        9,
        (units, part),
        (half,),
        w_down,
        w_up,
        w_out,
        short_w,
        conv_bias,
        gain_mlp[None],
        *tables,
    )
    near = lax.ppermute(sent, ("z", "h"), other_half_pairs())
    far = lax.ppermute(near[: width * blocks * 3 // 2], ("y", "x", "c"), neighbour_pairs())
    mixed = call(
        channel_kernel,
        shape((shards, samples), jnp.bfloat16),
        2**29,
        mine,
        short_w,
        conv_bias,
        arrived.transpose(1, 0, 2),
        *tables,
        scalars=1,
    )
    doubled = jnp.concatenate([mixed, mixed], axis=0)
    returned = lax.all_to_all(
        doubled,
        ("h",) + SEQ,
        split_axis=0,
        concat_axis=0,
        tiled=True,
        axis_index_groups=[second_ranks(DEEP, HIGH, WIDE)],
    )
    partial = call(
        out_kernel,
        shape((samples, blocks * width), jnp.bfloat16),
        2**31,
        half,
        returned.reshape(2, shards, samples),
        w_out,
        near,
        scalars=1,
    )
    shares = lax.all_gather(partial, "c", axis=0)
    own, normed, partial = call(
        mlp_kernel,
        (
            shape((samples, width), jnp.bfloat16),
            shape((samples, blocks * width), jnp.bfloat16),
            shape((samples, part), jnp.float32),
        ),
        2**28,
        place,
        whole,
        shares,
        gain_mlp,
        w_up,
        w_down,
        near,
        scalars=1,
    )
    pieces = call(
        far_kernel, shape((2, samples, width), jnp.bfloat16), 2**27, normed, partial, far
    )
    pieces = lax.all_gather(pieces, "c", axis=0)
    pieces = lax.dynamic_index_in_dim(pieces, place[0] % 2, 1, keepdims=False)
    total = jnp.sum(pieces.astype(jnp.float32), axis=0)
    return (own.astype(jnp.float32) + total).astype(jnp.bfloat16)


def solution(mesh):
    fine = Mesh(mesh.devices.reshape(4, 8, 4, 2, 2), SEQ + CH)
    return jax.shard_map(
        local,
        mesh=fine,
        in_specs=(
            P(SEQ, CH),
            P(),
            P(None, None, CH),
            P(None, None, CH),
            P(None, CH, SEQ),
            P(None, CH),
            P(CH, None),
            P(),
            P(None, CH),
            P(CH, None),
        ),
        out_specs=P(SEQ, CH),
        check_vma=False,
    )
```

```python
import jax
import jax.numpy as jnp
import ml_dtypes
import numpy as np
from jax import lax
from jax.experimental import pallas as pl
from jax.experimental.pallas import tpu as pltpu
from jax.sharding import Mesh, PartitionSpec as P

epsilon = 1e-06

SEQ = ("z", "y", "x")
CH = ("h", "c")
DEEP, HIGH, WIDE = 4, 8, 4


def rms_norm(values, gain):
    wide = values.astype(jnp.float32)
    scale = lax.rsqrt(jnp.mean(wide * wide, axis=-1, keepdims=True) + epsilon)
    return (wide * scale * gain).astype(jnp.bfloat16)


def halves_of(table):
    high = table.astype(ml_dtypes.bfloat16)
    low = (table - high.astype(np.float64)).astype(ml_dtypes.bfloat16)
    return high, low


def first_ranks(deep, high, wide):
    def nearness(place):
        y = abs(place // wide % high - high // 2)
        x = abs(place % wide - (wide - 1))
        z = deep - 1 - place // (high * wide)
        return -(z + min(y, high - y) + min(x, wide - x))

    last = ((deep - 1) * high + high // 2) * wide + wide - 1
    rest = [place for place in range(deep * high * wide) if place != last]
    return [last] + sorted(rest, key=nearness)


def second_ranks(deep, high, wide):
    ranks = first_ranks(deep, high, wide)
    return [len(ranks) + rank for rank in ranks] + ranks


def previous_rows(times):
    times = np.asarray(times)
    return (times[:, None] == times[None, :] + 1).astype(ml_dtypes.bfloat16)


def transform_tables(rows, cols, times):
    size = rows * cols
    times = np.asarray(times)
    row = np.arange(rows, dtype=np.float64)
    col = np.arange(cols, dtype=np.float64)
    outer_angle = 2.0 * np.pi * (((row[:, None] + 0.25) * row[None, :]) % rows) / rows
    inner_angle = 2.0 * np.pi * ((col[:, None] * col[None, :]) % cols) / cols
    turn_angle = 2.0 * np.pi * (row[:, None] + 0.25) * col[None, :] / size
    outer = np.concatenate([np.cos(outer_angle), -np.sin(outer_angle)], axis=0)
    cos, sin = np.cos(inner_angle), np.sin(inner_angle)
    inner = np.block([[cos, -sin], [sin, cos]])
    outer = outer[:, times]
    outer_high, outer_low = halves_of(outer)
    inner_high, inner_low = halves_of(inner)
    back_high, back_low = halves_of(outer.T / size)
    products = [np.concatenate([outer_high, outer_low], axis=1)]
    products += [inner_high, inner_low, np.concatenate([back_high, back_low], axis=0)]
    turn = np.stack([np.cos(turn_angle), -np.sin(turn_angle)])
    return np.stack(products), turn.astype(np.float32)


def dot(left, right):
    return jnp.dot(left, right, preferred_element_type=jnp.float32)


def split(values):
    high = values.astype(jnp.bfloat16)
    return high, (values - high.astype(jnp.float32)).astype(jnp.bfloat16)


def dot_split(values, high_table, low_table):
    high, low = split(values)
    rows = values.shape[0]
    both = dot(jnp.concatenate([high, low], axis=0), high_table)
    return both[:rows] + both[rows:] + dot(high, low_table)


def delayed(values, above, by):
    col = lax.broadcasted_iota(jnp.int32, values.shape, 1)
    return jnp.where(col >= by, pltpu.roll(values, by, 1), pltpu.roll(above, by, 1))


def round_bf16(values):
    return values.astype(jnp.bfloat16).astype(jnp.float32)


def channel_kernel(mine, short_w, bias, u, previous, products, turn, mixed):
    rows, cols = u.shape[1], u.shape[2] // 3
    projected = u[0]
    above = dot(previous[...], projected)
    outer, inner_high, inner_low = products[0], products[1], products[2]
    back_high, back_low = products[3, :rows], products[3, rows:]
    turn_real, turn_imag = turn[0], turn[1]
    per_channel = jnp.concatenate([short_w[k] for k in range(short_w.shape[0])] + [bias[...]], axis=0)
    column = lax.broadcasted_iota(jnp.int32, per_channel.shape, 1)
    scalars = jnp.sum(jnp.where(column == mine[0], per_channel, 0.0), axis=1, keepdims=True)
    scalars = [scalars[k : k + 1] for k in range(scalars.shape[0])]

    def short(k):
        values = projected[:, k * cols : (k + 1) * cols].astype(jnp.float32)
        total = scalars[3 * k] * values
        past = above[:, k * cols : (k + 1) * cols]
        total = total + scalars[3 * k + 1] * delayed(values, past, 1)
        total = total + scalars[3 * k + 2] * delayed(values, past, 2)
        return total.astype(jnp.bfloat16)

    def forward(signals):
        count = len(signals)
        side = jnp.concatenate(signals, axis=1) if count > 1 else signals[0]
        first = dot(outer, jnp.concatenate([side, side], axis=0))
        turned = []
        for k in range(count):
            real = first[:rows, k * cols : (k + 1) * cols]
            imag = first[rows:, k * cols : (k + 1) * cols]
            turned.append(
                jnp.concatenate(
                    [
                        real * turn_real - imag * turn_imag,
                        real * turn_imag + imag * turn_real,
                    ],
                    axis=1,
                )
            )
        stacked = jnp.concatenate(turned, axis=0) if count > 1 else turned[0]
        spectra = dot_split(stacked, inner_high, inner_low)
        return [
            (spectra[k * rows : (k + 1) * rows, :cols], spectra[k * rows : (k + 1) * rows, cols:])
            for k in range(count)
        ]

    def inverse(one, two):
        real = one[0] * two[0] - one[1] * two[1]
        negated = -one[0] * two[1] - one[1] * two[0]
        inner = dot_split(
            jnp.concatenate([real, negated], axis=1), inner_high, inner_low
        )
        real, negated = inner[:, :cols], inner[:, cols:]
        turned = jnp.concatenate(
            [
                real * turn_real - negated * turn_imag,
                -negated * turn_real - real * turn_imag,
            ],
            axis=0,
        )
        high, low = split(turned)
        side = dot(back_high, jnp.concatenate([high, low], axis=1))
        return side[:, :cols] + side[:, cols:] + dot(back_low, high)

    v = short(0)
    signal, response_one, response_two = forward([v, u[1, :, :cols], u[1, :, cols : 2 * cols]])
    first = inverse(signal, response_one) + scalars[9] * v.astype(jnp.float32)
    gated = (short(1).astype(jnp.float32) * round_bf16(first)).astype(jnp.bfloat16)
    (signal,) = forward([gated])
    second = inverse(signal, response_two) + scalars[10] * gated.astype(jnp.float32)
    mixed[...] = (short(2).astype(jnp.float32) * round_bf16(second)).astype(jnp.bfloat16)


def call(
    kernel, out_shape, flops, *operands, scalars=0, source=pltpu.VMEM, scratch=(), limit=16
):
    vmem = pl.BlockSpec(memory_space=pltpu.VMEM)
    smem = pl.BlockSpec(memory_space=pltpu.SMEM)
    held = pl.BlockSpec(memory_space=source)
    return pl.pallas_call(
        kernel,
        out_shape=out_shape,
        in_specs=[smem] * scalars + [held] * (len(operands) - scalars),
        out_specs=jax.tree.map(lambda _: vmem, out_shape),
        scratch_shapes=scratch,
        compiler_params=pltpu.CompilerParams(vmem_limit_bytes=limit * 2**20),
        cost_estimate=pl.CostEstimate(flops=flops, bytes_accessed=2**20, transcendentals=0),
    )(*operands)


def copy_all(pairs, sems):
    copies = [
        pltpu.make_async_copy(source, target, sems.at[k])
        for k, (source, target) in enumerate(pairs)
    ]
    for copy in copies:
        copy.start()
    for copy in copies:
        copy.wait()


def first_load_kernel(half, parity, *refs):
    count = (len(refs) + 1) // 2
    sources, (sent, *held), sems = refs[:count], refs[count:-1], refs[-1]
    w_up, w_down, w_out = sources[:3]
    units, wide = w_up.shape
    rows = w_out.shape[0]
    part = wide // 2
    there = pl.ds(pl.multiple_of((1 - half[0]) * part, part), part)
    turn = pl.ds(pl.multiple_of(parity[0] * part, part), part)
    pairs = [
        (w_up.at[:, turn], sent.at[pl.ds(0, units)]),
        (w_down.at[turn, there], sent.at[pl.ds(units, part)]),
        (w_out.at[:, pl.ds(0, part)], sent.at[pl.ds(units + part, rows)]),
        (w_out.at[:, pl.ds(part, part)], sent.at[pl.ds(units + part + rows, rows)]),
    ]
    copy_all(pairs + list(zip(sources[3:], held)), sems)


def last_load_kernel(half, w_down, *refs):
    count = (len(refs) - 2) // 2
    sources, (down, *held), sems = refs[:count], refs[count:-1], refs[-1]
    part = down.shape[1]
    here = pl.ds(pl.multiple_of(half[0] * part, part), part)
    copy_all([(w_down.at[:, here], down)] + list(zip(sources, held)), sems)


def load(kernel, copies, cut, scalars, *arrays):
    arrays = [pltpu.with_memory_space_constraint(array, pltpu.HBM) for array in arrays]
    held = [pltpu.VMEM(cut, jnp.bfloat16)]
    held += [pltpu.VMEM(array.shape, array.dtype) for array in arrays[-(copies - 1) :]]
    sems = [pltpu.SemaphoreType.DMA((len(arrays) + 1,))]
    return call(
        kernel,
        held,
        0,
        *scalars,
        *arrays,
        scalars=len(scalars),
        source=pltpu.HBM,
        scratch=sems,
    )


def project_kernel(whole, gain, w_in, filters, outgoing):
    normed = rms_norm(whole[...], gain[...])
    count, _, width = w_in.shape
    for k in range(count):
        outgoing[0, :, k * width : (k + 1) * width] = lax.dot_general(
            w_in[k], normed, (((0,), (1,)), ((), ())), preferred_element_type=jnp.float32
        ).astype(jnp.bfloat16)
    outgoing[1] = jnp.concatenate([filters[0], filters[1], jnp.zeros_like(filters[0])], axis=1)


def out_kernel(half, arrived, own, near, partial):
    rows = arrived.shape[1]
    first = near.shape[0] - 2 * rows
    other = jnp.concatenate([near[first : first + rows], near[first + rows :]], axis=1)
    low = half[0] == 0
    weights = (jnp.where(low, own[...], other), jnp.where(low, other, own[...]))
    parts = [
        lax.dot_general(
            arrived[1 - k],
            weights[k],
            (((0,), (0,)), ((), ())),
            preferred_element_type=jnp.float32,
        )
        for k in range(2)
    ]
    partial[...] = parts[0] + parts[1]


def mlp_kernel(place, whole, shares, gain, w_up, w_down, near, own, normed, partial):
    units = whole.shape[1]
    width = own.shape[1]
    half_units = units // 2
    share = shares[0] + shares[1]
    middle = (whole[...].astype(jnp.float32) + share).astype(jnp.bfloat16)
    mine = middle[:, :width]
    for k in range(1, units // width):
        mine = jnp.where(place[0] == k, middle[:, k * width : (k + 1) * width], mine)
    own[...] = mine
    scaled = rms_norm(middle, gain[...])
    normed[...] = scaled
    hidden = jax.nn.gelu(dot(scaled, w_up[...])).astype(jnp.bfloat16)
    total = dot(hidden, w_down[...])
    hidden = jax.nn.gelu(dot(scaled, near[:units])).astype(jnp.bfloat16)
    partial[...] = total + dot(hidden, near[units : units + half_units])


def far_kernel(normed, partial, far, pieces):
    count, _, width = pieces.shape
    units = normed.shape[1]
    hidden = jax.nn.gelu(dot(normed[...], far[:units])).astype(jnp.bfloat16)
    total = (partial[...] + dot(hidden, far[units:])).astype(jnp.bfloat16)
    for k in range(count):
        pieces[k] = total[:, k * width : (k + 1) * width]


def other_half_pairs():
    pairs = []
    for z in range(8):
        there = (z + 2) % 8
        if there // 4 == z // 4:
            there = (z - 2) % 8
        pairs.append((z % 4 * 2 + z // 4, there % 4 * 2 + there // 4))
    return pairs


def neighbour_pairs():
    high, wide = lax.axis_size("y"), lax.axis_size("x")
    pairs = []
    for y in range(high):
        for x in range(wide):
            pairs.append(((y * wide + x) * 2, ((y ^ 1) * wide + x) * 2))
            pairs.append(((y * wide + x) * 2 + 1, (y * wide + (x ^ 1)) * 2 + 1))
    return pairs


def local(tokens, gain_mix, w_in, short_w, filters, conv_bias, w_out, gain_mlp, w_up, w_down):
    samples, width = tokens.shape
    shards = lax.axis_size(SEQ)
    blocks = lax.axis_size(CH)
    shape = jax.ShapeDtypeStruct
    ranks = first_ranks(deep, high, wide)
    return [len(ranks) + rank for rank in ranks] + ranks


def previous_rows(times):
    times = np.asarray(times)
    return (times[:, None] == times[None, :] + 1).astype(ml_dtypes.bfloat16)


def transform_tables(rows, cols, times):
    size = rows * cols
    times = np.asarray(times)
    row = np.arange(rows, dtype=np.float64)
    col = np.arange(cols, dtype=np.float64)
    outer_angle = 2.0 * np.pi * (((row[:, None] + 0.25) * row[None, :]) % rows) / rows
    inner_angle = 2.0 * np.pi * ((col[:, None] * col[None, :]) % cols) / cols
    turn_angle = 2.0 * np.pi * (row[:, None] + 0.25) * col[None, :] / size
    outer = np.concatenate([np.cos(outer_angle), -np.sin(outer_angle)], axis=0)
    cos, sin = np.cos(inner_angle), np.sin(inner_angle)
    inner = np.block([[cos, -sin], [sin, cos]])
    outer = outer[:, times]
    outer_high, outer_low = halves_of(outer)
    inner_high, inner_low = halves_of(inner)
    back_high, back_low = halves_of(outer.T / size)
    products = [np.concatenate([outer_high, outer_low], axis=1)]
    products += [inner_high, inner_low, np.concatenate([back_high, back_low], axis=0)]
    turn = np.stack([np.cos(turn_angle), -np.sin(turn_angle)])
    return np.stack(products), turn.astype(np.float32)


def dot(left, right):
    return jnp.dot(left, right, preferred_element_type=jnp.float32)


def split(values):
    high = values.astype(jnp.bfloat16)
    return high, (values - high.astype(jnp.float32)).astype(jnp.bfloat16)


def dot_split(values, high_table, low_table):
    high, low = split(values)
    rows = values.shape[0]
    both = dot(jnp.concatenate([high, low], axis=0), high_table)
    return both[:rows] + both[rows:] + dot(high, low_table)


def delayed(values, above, by):
    col = lax.broadcasted_iota(jnp.int32, values.shape, 1)
    return jnp.where(col >= by, pltpu.roll(values, by, 1), pltpu.roll(above, by, 1))


def round_bf16(values):
    return values.astype(jnp.bfloat16).astype(jnp.float32)


def channel_kernel(mine, short_w, bias, u, previous, products, turn, mixed):
    rows, cols = u.shape[1], u.shape[2] // 3
    projected = u[0]
    above = dot(previous[...], projected)
    outer, inner_high, inner_low = products[0], products[1], products[2]
    back_high, back_low = products[3, :rows], products[3, rows:]
    turn_real, turn_imag = turn[0], turn[1]
    per_channel = jnp.concatenate([short_w[k] for k in range(short_w.shape[0])] + [bias[...]], axis=0)
    column = lax.broadcasted_iota(jnp.int32, per_channel.shape, 1)
    scalars = jnp.sum(jnp.where(column == mine[0], per_channel, 0.0), axis=1, keepdims=True)
    scalars = [scalars[k : k + 1] for k in range(scalars.shape[0])]

    def short(k):
        values = projected[:, k * cols : (k + 1) * cols].astype(jnp.float32)
        total = scalars[3 * k] * values
        past = above[:, k * cols : (k + 1) * cols]
        total = total + scalars[3 * k + 1] * delayed(values, past, 1)
        total = total + scalars[3 * k + 2] * delayed(values, past, 2)
        return total.astype(jnp.bfloat16)

    def forward(signals):
        count = len(signals)
        side = jnp.concatenate(signals, axis=1) if count > 1 else signals[0]
        first = dot(outer, jnp.concatenate([side, side], axis=0))
        turned = []
        for k in range(count):
            real = first[:rows, k * cols : (k + 1) * cols]
            imag = first[rows:, k * cols : (k + 1) * cols]
            turned.append(
                jnp.concatenate(
                    [
                        real * turn_real - imag * turn_imag,
                        real * turn_imag + imag * turn_real,
                    ],
                    axis=1,
                )
            )
        stacked = jnp.concatenate(turned, axis=0) if count > 1 else turned[0]
        spectra = dot_split(stacked, inner_high, inner_low)
        return [
            (spectra[k * rows : (k + 1) * rows, :cols], spectra[k * rows : (k + 1) * rows, cols:])
            for k in range(count)
        ]

    def inverse(one, two):
        real = one[0] * two[0] - one[1] * two[1]
        negated = -one[0] * two[1] - one[1] * two[0]
        inner = dot_split(
            jnp.concatenate([real, negated], axis=1), inner_high, inner_low
        )
        real, negated = inner[:, :cols], inner[:, cols:]
        turned = jnp.concatenate(
            [
                real * turn_real - negated * turn_imag,
                -negated * turn_real - real * turn_imag,
            ],
            axis=0,
        )
        high, low = split(turned)
        side = dot(back_high, jnp.concatenate([high, low], axis=1))
        return side[:, :cols] + side[:, cols:] + dot(back_low, high)

    v = short(0)
    signal, response_one, response_two = forward([v, u[1, :, :cols], u[1, :, cols : 2 * cols]])
    first = inverse(signal, response_one) + scalars[9] * v.astype(jnp.float32)
    gated = (short(1).astype(jnp.float32) * round_bf16(first)).astype(jnp.bfloat16)
    (signal,) = forward([gated])
    second = inverse(signal, response_two) + scalars[10] * gated.astype(jnp.float32)
    mixed[...] = (short(2).astype(jnp.float32) * round_bf16(second)).astype(jnp.bfloat16)


def call(
    kernel, out_shape, flops, *operands, scalars=0, source=pltpu.VMEM, scratch=(), limit=16
):
    vmem = pl.BlockSpec(memory_space=pltpu.VMEM)
    smem = pl.BlockSpec(memory_space=pltpu.SMEM)
    held = pl.BlockSpec(memory_space=source)
    return pl.pallas_call(
        kernel,
        out_shape=out_shape,
        in_specs=[smem] * scalars + [held] * (len(operands) - scalars),
        out_specs=jax.tree.map(lambda _: vmem, out_shape),
        scratch_shapes=scratch,
        compiler_params=pltpu.CompilerParams(vmem_limit_bytes=limit * 2**20),
        cost_estimate=pl.CostEstimate(flops=flops, bytes_accessed=2**20, transcendentals=0),
    )(*operands)


def copy_all(pairs, sems):
    copies = [
        pltpu.make_async_copy(source, target, sems.at[k])
        for k, (source, target) in enumerate(pairs)
    ]
    for copy in copies:
        copy.start()
    for copy in copies:
        copy.wait()


def first_load_kernel(half, parity, *refs):
    count = (len(refs) + 1) // 2
    sources, (sent, *held), sems = refs[:count], refs[count:-1], refs[-1]
    w_up, w_down, w_out = sources[:3]
    units, wide = w_up.shape
    rows = w_out.shape[0]
    part = wide // 2
    there = pl.ds(pl.multiple_of((1 - half[0]) * part, part), part)
    turn = pl.ds(pl.multiple_of(parity[0] * part, part), part)
    pairs = [
        (w_up.at[:, turn], sent.at[pl.ds(0, units)]),
        (w_down.at[turn, there], sent.at[pl.ds(units, part)]),
        (w_out.at[:, pl.ds(0, part)], sent.at[pl.ds(units + part, rows)]),
        (w_out.at[:, pl.ds(part, part)], sent.at[pl.ds(units + part + rows, rows)]),
    ]
    copy_all(pairs + list(zip(sources[3:], held)), sems)


def last_load_kernel(half, w_down, *refs):
    count = (len(refs) - 2) // 2
    sources, (down, *held), sems = refs[:count], refs[count:-1], refs[-1]
    part = down.shape[1]
    here = pl.ds(pl.multiple_of(half[0] * part, part), part)
    copy_all([(w_down.at[:, here], down)] + list(zip(sources, held)), sems)


def load(kernel, copies, cut, scalars, *arrays):
    arrays = [pltpu.with_memory_space_constraint(array, pltpu.HBM) for array in arrays]
    held = [pltpu.VMEM(cut, jnp.bfloat16)]
    held += [pltpu.VMEM(array.shape, array.dtype) for array in arrays[-(copies - 1) :]]
    sems = [pltpu.SemaphoreType.DMA((len(arrays) + 1,))]
    return call(
        kernel,
        held,
        0,
        *scalars,
        *arrays,
        scalars=len(scalars),
        source=pltpu.HBM,
        scratch=sems,
    )


def project_kernel(whole, gain, w_in, filters, outgoing):
    normed = rms_norm(whole[...], gain[...])
    count, _, width = w_in.shape
    for k in range(count):
        outgoing[0, :, k * width : (k + 1) * width] = lax.dot_general(
            w_in[k], normed, (((0,), (1,)), ((), ())), preferred_element_type=jnp.float32
        ).astype(jnp.bfloat16)
    outgoing[1] = jnp.concatenate([filters[0], filters[1], jnp.zeros_like(filters[0])], axis=1)


def out_kernel(half, arrived, own, near, partial):
    rows = arrived.shape[1]
    first = near.shape[0] - 2 * rows
    other = jnp.concatenate([near[first : first + rows], near[first + rows :]], axis=1)
    low = half[0] == 0
    weights = (jnp.where(low, own[...], other), jnp.where(low, other, own[...]))
    parts = [
        lax.dot_general(
            arrived[1 - k],
            weights[k],
            (((0,), (0,)), ((), ())),
            preferred_element_type=jnp.float32,
        )
        for k in range(2)
    ]
    partial[...] = parts[0] + parts[1]


def mlp_kernel(place, whole, shares, gain, w_up, w_down, near, own, normed, partial):
    units = whole.shape[1]
    width = own.shape[1]
    half_units = units // 2
    share = shares[0] + shares[1]
    middle = (whole[...].astype(jnp.float32) + share).astype(jnp.bfloat16)
    mine = middle[:, :width]
    for k in range(1, units // width):
        mine = jnp.where(place[0] == k, middle[:, k * width : (k + 1) * width], mine)
    own[...] = mine
    scaled = rms_norm(middle, gain[...])
    normed[...] = scaled
    hidden = jax.nn.gelu(dot(scaled, w_up[...])).astype(jnp.bfloat16)
    total = dot(hidden, w_down[...])
    hidden = jax.nn.gelu(dot(scaled, near[:units])).astype(jnp.bfloat16)
    partial[...] = total + dot(hidden, near[units : units + half_units])


def far_kernel(normed, partial, far, pieces):
    count, _, width = pieces.shape
    units = normed.shape[1]
    hidden = jax.nn.gelu(dot(normed[...], far[:units])).astype(jnp.bfloat16)
    total = (partial[...] + dot(hidden, far[units:])).astype(jnp.bfloat16)
    for k in range(count):
        pieces[k] = total[:, k * width : (k + 1) * width]


def other_half_pairs():
    pairs = []
    for z in range(8):
        there = (z + 2) % 8
        if there // 4 == z // 4:
            there = (z - 2) % 8
        pairs.append((z % 4 * 2 + z // 4, there % 4 * 2 + there // 4))
    return pairs


def neighbour_pairs():
    high, wide = lax.axis_size("y"), lax.axis_size("x")
    pairs = []
    for y in range(high):
        for x in range(wide):
            pairs.append(((y * wide + x) * 2, ((y ^ 1) * wide + x) * 2))
            pairs.append(((y * wide + x) * 2 + 1, (y * wide + (x ^ 1)) * 2 + 1))
    return pairs


def local(tokens, gain_mix, w_in, short_w, filters, conv_bias, w_out, gain_mlp, w_up, w_down):
    samples, width = tokens.shape
    shards = lax.axis_size(SEQ)
    blocks = lax.axis_size(CH)
    shape = jax.ShapeDtypeStruct
    place_z, place_y, place_x = (lax.axis_index(axis) for axis in SEQ)
    mine = (DEEP - 1 - place_z) * HIGH + (place_y + HIGH // 2) % HIGH
    mine = (mine * WIDE + (place_x + 1) % WIDE).astype(jnp.int32)[None]
    ranks = first_ranks(DEEP, HIGH, WIDE)
    mine = jnp.asarray(np.argsort(ranks).astype(np.int32))[lax.axis_index(SEQ)][None]
    place = lax.axis_index(CH).astype(jnp.int32)[None]
    half = lax.axis_index("h").astype(jnp.int32)[None]
    side = jnp.where(lax.axis_index("c") == 0, lax.axis_index("y"), lax.axis_index("x"))
    parity = (side % 2).astype(jnp.int32)[None]
    tables = [previous_rows(ranks), *transform_tables(shards, samples, ranks)]
    tables = [jnp.asarray(table) for table in tables]
    units, wide = w_up.shape
    part = wide // 2
    sent, tokens, gain_mix, w_in, filters = load(
        first_load_kernel,
        5,
        (units + part + 2 * width, part),
        (half, parity),
        w_up,
        w_down,
        w_out,
        tokens,
        gain_mix[None],
        w_in,
        filters,
    )
    whole = lax.all_gather(tokens, CH, axis=1, tiled=True)
    outgoing = call(
        project_kernel,
        shape((2, width, 3 * samples), jnp.bfloat16),
        2**26,
        whole,
        gain_mix,
        w_in,
        filters,
    )
    outgoing, sent, half, parity, place, w_up = lax.optimization_barrier(
        (outgoing.transpose(1, 0, 2), sent, half, parity, place, w_up)
    )
    arrived = lax.all_to_all(
        outgoing, SEQ, split_axis=0, concat_axis=0, tiled=True, axis_index_groups=[ranks]
    )
    w_down, w_up, w_out, short_w, conv_bias, gain_mlp, *tables = load(
        last_load_kernel,
        9,
        (units, part),
        (half,),
        w_down,
        w_up,
        w_out,
        short_w,
        conv_bias,
        gain_mlp[None],
        *tables,
    )
    near = lax.ppermute(sent, ("z", "h"), other_half_pairs())
    far = lax.ppermute(near[: width * blocks * 3 // 2], ("y", "x", "c"), neighbour_pairs())
    mixed = call(
        channel_kernel,
        shape((shards, samples), jnp.bfloat16),
        2**29,
        mine,
        short_w,
        conv_bias,
        arrived.transpose(1, 0, 2),
        *tables,
        scalars=1,
    )
    doubled = jnp.concatenate([mixed, mixed], axis=0)
    returned = lax.all_to_all(
        doubled,
        ("h",) + SEQ,
        split_axis=0,
        concat_axis=0,
        tiled=True,
        axis_index_groups=[second_ranks(DEEP, HIGH, WIDE)],
    )
    partial = call(
        out_kernel,
        shape((samples, blocks * width), jnp.float32),
        2**31,
        half,
        returned.reshape(2, shards, samples),
        w_out,
        near,
        scalars=1,
    )
    shares = lax.all_gather(partial, "c", axis=0)
    own, normed, partial = call(
        mlp_kernel,
        (
            shape((samples, width), jnp.bfloat16),
            shape((samples, blocks * width), jnp.bfloat16),
            shape((samples, part), jnp.float32),
        ),
        2**28,
        place,
        whole,
        shares,
        gain_mlp,
        w_up,
        w_down,
        near,
        scalars=1,
    )
    pieces = call(
        far_kernel, shape((2, samples, width), jnp.bfloat16), 2**27, normed, partial, far
    )
    pieces = lax.all_gather(pieces, "c", axis=0)
    pieces = lax.dynamic_index_in_dim(pieces, place[0] % 2, 1, keepdims=False)
    total = jnp.sum(pieces.astype(jnp.float32), axis=0)
    return (own.astype(jnp.float32) + total).astype(jnp.bfloat16)


def solution(mesh):
    fine = Mesh(mesh.devices.reshape(4, 8, 4, 2, 2), SEQ + CH)
    return jax.shard_map(
        local,
        mesh=fine,
        in_specs=(
            P(SEQ, CH),
            P(),
            P(None, None, CH),
            P(None, None, CH),
            P(None, CH, SEQ),
            P(None, CH),
            P(CH, None),
            P(),
            P(None, CH),
            P(CH, None),
        ),
        out_specs=P(SEQ, CH),
        check_vma=False,
    )
```
